256 devices in a mesh: dp: 16 (over z, core), node: 4 (over x), pipe: 4 (over y).
Axes of the slice: x: 4, y: 4, z: 8, core: 2. Of those that a mesh axis runs over, the one named last changes fastest.
Arguments:
- final_hidden: bfloat16 [32768, 8192], P(('dp', 'node', 'pipe')), may hold values from -128 to 128
- value_head: bfloat16 [8192, 128], replicated, may hold values from -3 to 3
- norm_gain: bfloat16 [8192], replicated, may hold values from 0.5 to 1.5
- rewards: float32 [32768], P(('dp', 'node', 'pipe')), may hold values from -6 to 6
- old_values: float32 [32768], P(('dp', 'node', 'pipe')), may hold values from -6 to 6
- loss_mask: int32 [32768], P(('dp', 'node', 'pipe')), may hold values 0 or 1
- row_exp: int32 [256, 8192], P(('dp', 'node', 'pipe')), may hold values from -14 to -11
- gain_exp: int32 [256, 64], P(('dp', 'node', 'pipe')), may hold values from -16 to -7
- first_w: float32 [8192, 128], P(('dp', 'node', 'pipe')), may hold values from -4 to 4
- second_w: float32 [8192, 128], P(('dp', 'node', 'pipe')), may hold values from 0.01 to 1
- first_g: float32 [8192], P(('dp', 'node', 'pipe')), may hold values from -4 to 4
- second_g: float32 [8192], P(('dp', 'node', 'pipe')), may hold values from 0.01 to 1
Outputs:
- new_weight: bfloat16 [8192, 128], P(('dp', 'node'))
- new_gain: bfloat16 [8192], P(('dp', 'node'))
- first_w_new: float32 [8192, 128], P(('dp', 'node', 'pipe'))
- second_w_new: float32 [8192, 128], P(('dp', 'node', 'pipe'))
- first_g_new: float32 [8192], P(('dp', 'node', 'pipe'))
- second_g_new: float32 [8192], P(('dp', 'node', 'pipe'))
The draws below stay inside these ranges and needn't reach their ends.
All inputs are finite; a program needn't handle non-finite values. No bound on the sum of `loss_mask` on one device may be relied on, other than what follows from the above.
Results may differ from the reference program's by a relative error of at most 0.0055.
Values may be sent and summed in bfloat16 or wider, within the bound.
No kernel may reach another device: no remote copies, remote signals or barrier semaphores. Data moves between devices by JAX's collectives and lax.ppermute only.
A program may use at most 64 MiB of HBM per device.

```python
import math
import jax
import jax.numpy as jnp
from jax import lax

D = 8192
BINS = 128
GBLK = 128
SEQ = 32
T_DEV = 128
GROUPS = 256
TOKENS = 32768
N_DP = 16
N_NODE = 4
N_PIPE = 4


def head_columns(key):
    return 0.4 * jax.random.truncated_normal(jax.random.fold_in(key, 101), -6.0, 6.0, (D, BINS), jnp.float32)


def draw_value_head(key, part):
    return head_columns(key).astype(jnp.bfloat16)


def draw_final_hidden(key, part):
    drawn = jax.random.truncated_normal(jax.random.fold_in(key, 202), -6.0, 6.0, (TOKENS, D), jnp.float32)
    return drawn.astype(jnp.bfloat16)


def touch_ends(values, key, low, high):
    extent = values.shape
    spot = [jax.random.randint(jax.random.fold_in(key, axis), (), 0, extent[axis]) for axis in range(len(extent))]
    values = values.at[tuple(spot)].set(low)
    longest = extent.index(max(extent))
    spot[longest] = (spot[longest] + 1) % extent[longest]
    return values.at[tuple(spot)].set(high)


def level_of(rng, extent, cuts, low, largest):
    def one(position, blocks):
        draws = jax.random.uniform(jax.random.fold_in(jax.random.fold_in(rng, 6), position), (blocks,), jnp.float32, low / len(cuts), largest / len(cuts))
        return jnp.repeat(jnp.exp(draws), extent[position] // blocks).reshape((-1,) + (1,) * (len(extent) - position - 1))

    factor_of = one(*cuts[0])
    for cut in cuts[1:]:
        factor_of = factor_of * one(*cut)
    return factor_of


def scatter_about(own_key, extent, scale, limit, split=(), dtype=jnp.bfloat16):
    entries = scale * jax.random.normal(own_key, extent, jnp.float32)
    if split:
        entries = entries * level_of(own_key, extent, split, -0.22, 0.18)
    return jnp.clip(entries, -limit, limit).astype(dtype)


def setup_inputs(seed: int = 0) -> dict:
    seeds = jax.random.split(jax.random.key(seed), 13)
    final_hidden = draw_final_hidden(jax.random.fold_in(seeds[12], 71), 0)
    value_head = draw_value_head(jax.random.fold_in(seeds[12], 71), 0)
    norm_gain = jnp.clip(1.0 + 0.1 * jax.random.normal(seeds[2], (D,), jnp.float32), 0.5, 1.5).astype(jnp.bfloat16)
    rewards = scatter_about(seeds[3], (TOKENS,), 0.5, 6.0, ((0, 256),), jnp.float32)
    old_values = scatter_about(seeds[4], (TOKENS,), 0.5, 6.0, ((0, 256),), jnp.float32)
    loss_mask = touch_ends((jax.random.randint(seeds[5], (TOKENS,), 0, 4) < 3).astype(jnp.int32), jax.random.fold_in(seeds[5], 1), 0, 1)
    row_exp = touch_ends(jax.random.randint(seeds[6], (GROUPS, D), -14, -10), jax.random.fold_in(seeds[6], 1), -14, (-10) - 1).astype(jnp.int32)
    gain_exp = touch_ends(jax.random.randint(seeds[7], (GROUPS, D // GBLK), -16, -6), jax.random.fold_in(seeds[7], 1), -16, (-6) - 1).astype(jnp.int32)
    first_w = scatter_about(seeds[8], (D, BINS), 0.3, 4.0, ((0, 256),), jnp.float32)
    second_w = jnp.clip(jnp.exp(math.log(1.0) - 4.6051702 * jax.random.uniform(seeds[9], (D, BINS), jnp.float32) ** level_of(seeds[9], (D, BINS), ((0, 256),), -0.2, 0.2)), 0.01, 1.0)
    first_g = scatter_about(seeds[10], (D,), 0.3, 4.0, ((0, 256),), jnp.float32)
    second_g = jnp.clip(jnp.exp(math.log(1.0) - 4.6051702 * jax.random.uniform(seeds[11], (D,), jnp.float32) ** level_of(seeds[11], (D,), ((0, 256),), -0.2, 0.2)), 0.01, 1.0)
    return {"final_hidden": final_hidden, "value_head": value_head, "norm_gain": norm_gain, "rewards": rewards, "old_values": old_values, "loss_mask": loss_mask, "row_exp": row_exp, "gain_exp": gain_exp, "first_w": first_w, "second_w": second_w, "first_g": first_g, "second_g": second_g}


LOGIT_SCALE = 0.0625
RETURN_LOW = -4.0
RETURN_HIGH = 4.0
TRACE_DECAY = 0.95
SAT_LIMIT = 448.0
LEARN_RATE = 0.02
FIRST_CORR = 0.19
SECOND_CORR = 0.0975
EPSILON = 1e-08
NORM_EPSILON = 1e-06

def gauss_targets(returns):
    width = (RETURN_HIGH - RETURN_LOW) / BINS
    spread = 0.75 * width
    bin_edges = RETURN_LOW + width * jnp.arange(BINS + 1).astype(jnp.float32)
    clamped = jnp.clip(returns, RETURN_LOW, RETURN_HIGH)
    cum_mass = 0.5 * (1.0 + jax.scipy.special.erf((bin_edges[None, :] - clamped[:, None]) / (spread * math.sqrt(2.0))))
    bin_mass = cum_mass[:, 1:] - cum_mass[:, :-1]
    return bin_mass / (cum_mass[:, -1:] - cum_mass[:, :1])

def gae_returns(rewards, old_values):
    reward_rows = rewards.reshape(-1, SEQ)
    value_rows = old_values.reshape(-1, SEQ)
    following = jnp.concatenate([value_rows[:, 1:], jnp.zeros((value_rows.shape[0], 1), jnp.float32)], axis=1)
    td_error = reward_rows + following - value_rows

    def backward(carry, column):
        carry = column + TRACE_DECAY * carry
        return (carry, carry)
    final_carry, traced = lax.scan(backward, jnp.zeros((value_rows.shape[0],), jnp.float32), td_error.T, reverse=True)
    return (traced.T + value_rows).reshape(-1)

def local_terms(hidden, gain, head, targets, mask, row_scale_exp, block_scale_exp):
    hidden_f = hidden.astype(jnp.float32)
    inv_rms = lax.rsqrt(lax.optimization_barrier(jnp.mean(hidden_f * hidden_f, axis=1, keepdims=True)) + NORM_EPSILON)
    normed = hidden_f * inv_rms
    scaled = (normed * gain.astype(jnp.float32)).astype(jnp.bfloat16)
    logits = LOGIT_SCALE * jnp.dot(scaled, head, preferred_element_type=jnp.float32)
    shifted = jnp.exp(logits - lax.optimization_barrier(jnp.max(logits, axis=1, keepdims=True)))
    probs_out = shifted / lax.optimization_barrier(jnp.sum(shifted, axis=1, keepdims=True))
    errors = (LOGIT_SCALE * mask.astype(jnp.float32)[:, None] * (probs_out - targets)).astype(jnp.bfloat16)
    weight_part = lax.dot_general(scaled, errors, (((0,), (0,)), ((), ())), preferred_element_type=jnp.float32)
    back_prop = lax.dot_general(errors, head, (((1,), (1,)), ((), ())), preferred_element_type=jnp.float32)
    gain_part = lax.optimization_barrier(jnp.sum(back_prop * normed, axis=0))
    row_limit = SAT_LIMIT * jnp.exp2(row_scale_exp.astype(jnp.float32))
    block_limit = SAT_LIMIT * jnp.repeat(jnp.exp2(block_scale_exp.astype(jnp.float32)), GBLK)
    weight_q = jnp.clip(weight_part, -row_limit[:, None], row_limit[:, None]).astype(jnp.bfloat16)
    gain_q = jnp.clip(gain_part, -block_limit, block_limit).astype(jnp.bfloat16)
    return lax.optimization_barrier((weight_q, gain_q))

def adam_update(param, grad, first, second):
    first_new = 0.9 * first + 0.1 * grad
    second_new = 0.95 * second + 0.05 * grad * grad
    update = first_new / FIRST_CORR / (jnp.sqrt(second_new / SECOND_CORR) + EPSILON)
    return ((param.astype(jnp.float32) - LEARN_RATE * update).astype(jnp.bfloat16), first_new, second_new)

def reference(final_hidden, value_head, norm_gain, rewards, old_values, loss_mask, row_exp, gain_exp, first_w, second_w, first_g, second_g):
    group_count = N_DP * N_NODE * N_PIPE
    targets = gauss_targets(gae_returns(rewards, old_values))

    def add_group(carry, group):
        start = group * T_DEV
        hidden = lax.dynamic_slice_in_dim(final_hidden, start, T_DEV, 0)
        group_targets = lax.dynamic_slice_in_dim(targets, start, T_DEV, 0)
        group_mask = lax.dynamic_slice_in_dim(loss_mask, start, T_DEV, 0)
        row_scale_exp = lax.dynamic_slice_in_dim(row_exp, group, 1, 0)[0]
        block_scale_exp = lax.dynamic_slice_in_dim(gain_exp, group, 1, 0)[0]
        weight_q, gain_q = local_terms(hidden, norm_gain, value_head, group_targets, group_mask, row_scale_exp, block_scale_exp)
        return ((carry[0] + weight_q.astype(jnp.float32), carry[1] + gain_q.astype(jnp.float32)), None)
    initial = (jnp.zeros((D, BINS), jnp.float32), jnp.zeros((D,), jnp.float32))
    totals, unused = lax.scan(add_group, initial, jnp.arange(group_count).astype(jnp.int32))
    new_weight, first_w_new, second_w_new = adam_update(value_head, totals[0], first_w, second_w)
    new_gain, first_g_new, second_g_new = adam_update(norm_gain, totals[1], first_g, second_g)
    return (new_weight, new_gain, first_w_new, second_w_new, first_g_new, second_g_new)
```

```python
import math

import jax
import jax.numpy as jnp
from jax import lax
from jax.sharding import PartitionSpec as P

BINS = 128
GBLK = 128
SEQ = 32


LOGIT_SCALE = 0.0625
RETURN_LOW = -4.0
RETURN_HIGH = 4.0
TRACE_DECAY = 0.95
SAT_LIMIT = 448.0
LEARN_RATE = 0.02
FIRST_CORR = 0.19
SECOND_CORR = 0.0975
EPSILON = 1e-08
NORM_EPSILON = 1e-06


def gauss_targets(returns):
    width = (RETURN_HIGH - RETURN_LOW) / BINS
    spread = 0.75 * width
    bin_edges = RETURN_LOW + width * jnp.arange(BINS + 1).astype(jnp.float32)
    clamped = jnp.clip(returns, RETURN_LOW, RETURN_HIGH)
    cum_mass = 0.5 * (
        1.0
        + jax.scipy.special.erf((bin_edges[None, :] - clamped[:, None]) / (spread * math.sqrt(2.0)))
    )
    bin_mass = cum_mass[:, 1:] - cum_mass[:, :-1]
    return bin_mass / (cum_mass[:, -1:] - cum_mass[:, :1])


def gae_returns(rewards, old_values):
    reward_rows = rewards.reshape(-1, SEQ)
    value_rows = old_values.reshape(-1, SEQ)
    following = jnp.concatenate(
        [value_rows[:, 1:], jnp.zeros((value_rows.shape[0], 1), jnp.float32)], axis=1
    )
    td_error = reward_rows + following - value_rows
    row_pos = lax.broadcasted_iota(jnp.int32, (SEQ, SEQ), 0)
    col_pos = lax.broadcasted_iota(jnp.int32, (SEQ, SEQ), 1)
    offset = jnp.maximum(row_pos - col_pos, 0).astype(jnp.float32)
    kernel = jnp.where(row_pos >= col_pos, jnp.power(TRACE_DECAY, offset), 0.0)
    traced = jnp.dot(td_error, kernel, precision=lax.Precision.HIGHEST)
    return (traced + value_rows).reshape(-1)


def forward(hidden, gain, head, targets, mask):
    hidden_f = hidden.astype(jnp.float32)
    inv_rms = lax.rsqrt(jnp.mean(hidden_f * hidden_f, axis=1, keepdims=True) + NORM_EPSILON)
    scaled = (hidden_f * inv_rms * gain.astype(jnp.float32)).astype(jnp.bfloat16)
    logits = LOGIT_SCALE * jnp.dot(scaled, head, preferred_element_type=jnp.float32)
    shifted = jnp.exp(logits - jnp.max(logits, axis=1, keepdims=True))
    probs_out = shifted / jnp.sum(shifted, axis=1, keepdims=True)
    errors = (LOGIT_SCALE * mask.astype(jnp.float32)[:, None] * (probs_out - targets)).astype(
        jnp.bfloat16
    )
    return errors, inv_rms


def group_grads(hidden, inv_rms, errors, gain, head, row_scale_exp, block_scale_exp):
    normed = hidden.astype(jnp.float32) * inv_rms
    scaled = (normed * gain.astype(jnp.float32)).astype(jnp.bfloat16)
    weight_part = lax.dot_general(
        scaled, errors, (((0,), (0,)), ((), ())), preferred_element_type=jnp.float32
    )
    back_prop = lax.dot_general(
        errors, head, (((1,), (1,)), ((), ())), preferred_element_type=jnp.float32
    )
    gain_part = jnp.sum(back_prop * normed, axis=0)
    row_limit = SAT_LIMIT * jnp.exp2(row_scale_exp.astype(jnp.float32))
    block_limit = SAT_LIMIT * jnp.repeat(jnp.exp2(block_scale_exp.astype(jnp.float32)), GBLK)
    weight_q = jnp.clip(weight_part, -row_limit[:, None], row_limit[:, None]).astype(jnp.bfloat16)
    gain_q = jnp.clip(gain_part, -block_limit, block_limit).astype(jnp.bfloat16)
    return weight_q.astype(jnp.float32), gain_q.astype(jnp.float32)


def adam_update(param, grad, first, second):
    first_new = 0.9 * first + 0.1 * grad
    second_new = 0.95 * second + 0.05 * grad * grad
    update = first_new / FIRST_CORR / (jnp.sqrt(second_new / SECOND_CORR) + EPSILON)
    return (
        (param.astype(jnp.float32) - LEARN_RATE * update).astype(jnp.bfloat16),
        first_new,
        second_new,
    )


def shards(
    final_hidden,
    value_head,
    norm_gain,
    rewards,
    old_values,
    loss_mask,
    row_exp,
    gain_exp,
    first_w,
    second_w,
    first_g,
    second_g,
):
    size_dp = lax.axis_size("dp")
    size_node = lax.axis_size("node")
    size_pipe = lax.axis_size("pipe")
    size_z = size_dp // 2
    size_xy = size_node * size_pipe
    rows = first_g.shape[0]
    bins = value_head.shape[1]
    tokens = final_hidden.shape[0]
    core = lax.rem(lax.axis_index("dp"), 2)
    swap = [(i, i ^ 1) for i in range(size_dp)]
    same_core = [[c + 2 * i for i in range(size_z)] for c in range(2)]
    span = size_xy * rows

    def half(values, side):
        lead = values.shape[:-1]
        parts = values.reshape(*lead, size_z, 2, values.shape[-1] // (2 * size_z))
        return lax.dynamic_index_in_dim(parts, side, len(lead) + 1, keepdims=False).reshape(
            *lead, values.shape[-1] // 2
        )

    other_hidden = lax.ppermute(half(final_hidden, 1 - core), "dp", swap)
    other_row_exp = lax.ppermute(half(row_exp[0], 1 - core), "dp", swap)
    other_gain_exp = lax.ppermute(half(gain_exp[0], 1 - core), "dp", swap)

    targets = gauss_targets(gae_returns(rewards, old_values))
    errors, inv_rms = forward(final_hidden, norm_gain, value_head, targets, loss_mask)
    other_errors = lax.ppermute(errors, "dp", swap)
    other_rms = lax.ppermute(inv_rms, "dp", swap)

    own_gain = half(norm_gain, core)
    own_head = half(value_head.T, core).T
    mine = group_grads(
        half(final_hidden, core), inv_rms, errors, own_gain, own_head,
        half(row_exp[0], core), half(gain_exp[0], core),
    )
    theirs = group_grads(
        other_hidden, other_rms, other_errors, own_gain, own_head, other_row_exp, other_gain_exp
    )
    weight_pair = (mine[0] + theirs[0]).astype(jnp.bfloat16)
    weight_pair = weight_pair.reshape(size_z, size_xy, rows, bins).transpose(1, 0, 2, 3)
    weight_pair = weight_pair.reshape(size_xy, size_z * rows, bins)
    gain_pair = (mine[1] + theirs[1]).reshape(size_z, size_xy, rows).transpose(1, 0, 2)
    gain_pair = gain_pair.reshape(size_xy, size_z * rows // bins, bins)
    gain_high = gain_pair.astype(jnp.bfloat16)
    gain_low = (gain_pair - gain_high.astype(jnp.float32)).astype(jnp.bfloat16)
    filler = jnp.zeros((size_xy, 12, bins), jnp.bfloat16)
    packed = jnp.concatenate([weight_pair, gain_high, gain_low, filler], axis=1)
    packed = lax.all_to_all(packed, ("node", "pipe"), 0, 0, tiled=True)
    plane = jnp.sum(packed.astype(jnp.float32), axis=0)
    plane_w = plane[: size_z * rows].reshape(size_z, rows, bins)
    plane_g = plane[size_z * rows :][:2] + plane[size_z * rows :][2:4]
    plane_g = jnp.pad(plane_g.reshape(size_z, 1, rows), ((0, 0), (0, 7), (0, bins - rows)))
    packed = jnp.concatenate([plane_w, plane_g], axis=1)
    packed = lax.all_to_all(packed, "dp", 0, 0, tiled=True, axis_index_groups=same_core)
    total = jnp.sum(packed, axis=0)
    grad_w = total[:rows]
    grad_g = total[rows, :rows]

    position = (
        lax.axis_index("dp") * size_node + lax.axis_index("node")
    ) * size_pipe + lax.axis_index("pipe")
    own_weight = lax.dynamic_slice_in_dim(value_head, position * rows, rows, 0)
    own_gain = lax.dynamic_slice_in_dim(norm_gain, position * rows, rows, 0)
    shard_weight, first_w_new, second_w_new = adam_update(own_weight, grad_w, first_w, second_w)
    shard_gain, first_g_new, second_g_new = adam_update(own_gain, grad_g, first_g, second_g)
    packed = jnp.concatenate(
        [shard_weight, jnp.pad(shard_gain[None], ((0, 7), (0, bins - rows)))], axis=0
    )
    packed = lax.all_to_all(
        jnp.broadcast_to(packed, (size_pipe, *packed.shape)), "pipe", 0, 0, tiled=True
    )
    new_weight = packed[:, :rows].reshape(size_pipe * rows, bins)
    new_gain = packed[:, rows, :rows].reshape(size_pipe * rows)
    return (new_weight, new_gain, first_w_new, second_w_new, first_g_new, second_g_new)


def solution(mesh):
    return jax.shard_map(
        shards,
        mesh=mesh,
        in_specs=(
            P(("dp", "node", "pipe"), None),
            P(),
            P(),
            P(("dp", "node", "pipe")),
            P(("dp", "node", "pipe")),
            P(("dp", "node", "pipe")),
            P(("dp", "node", "pipe"), None),
            P(("dp", "node", "pipe"), None),
            P(("dp", "node", "pipe"), None),
            P(("dp", "node", "pipe"), None),
            P(("dp", "node", "pipe")),
            P(("dp", "node", "pipe")),
        ),
        out_specs=(
            P(("dp", "node"), None),
            P(("dp", "node")),
            P(("dp", "node", "pipe"), None),
            P(("dp", "node", "pipe"), None),
            P(("dp", "node", "pipe")),
            P(("dp", "node", "pipe")),
        ),
        check_vma=False,
    )
```

```python
import math

import jax
import jax.numpy as jnp
from jax import lax
from jax.experimental import pallas as pl
from jax.experimental.pallas import tpu as pltpu
from jax.sharding import PartitionSpec as P

BINS = 128
GBLK = 128
SEQ = 32


LOGIT_SCALE = 0.0625
RETURN_LOW = -4.0
RETURN_HIGH = 4.0
TRACE_DECAY = 0.95
SAT_LIMIT = 448.0
LEARN_RATE = 0.02
FIRST_CORR = 0.19
SECOND_CORR = 0.0975
EPSILON = 1e-08
NORM_EPSILON = 1e-06


LANES = 128
CHUNKS = 8
LIMIT_BASE = 16


def limit_of(exponent):
    power = jnp.left_shift(jnp.ones_like(exponent), exponent + LIMIT_BASE)
    return power.astype(jnp.float32) * (SAT_LIMIT * 2.0**-LIMIT_BASE)


def target_mass(rewards, old_values, tokens):
    width = (RETURN_HIGH - RETURN_LOW) / BINS
    scale = 0.75 * width * math.sqrt(2.0)
    token = lax.broadcasted_iota(jnp.int32, (tokens, tokens), 0)
    later = lax.broadcasted_iota(jnp.int32, (tokens, tokens), 1)
    values = jnp.broadcast_to(old_values, (tokens, tokens))
    following = jnp.where(lax.rem(later, SEQ) == SEQ - 1, 0.0, pltpu.roll(values, tokens - 1, 1))
    td_error = rewards + following - values
    behind = (later - token).astype(jnp.float32)
    inside = jnp.logical_and(later >= token, lax.div(later, SEQ) == lax.div(token, SEQ))
    decay = jnp.where(inside, jnp.exp(jnp.maximum(behind, 0.0) * math.log(TRACE_DECAY)), 0.0)
    own = jnp.where(later == token, values, 0.0)
    returns = jnp.sum(decay * td_error + own, axis=1, keepdims=True)
    returns = jnp.clip(returns, RETURN_LOW, RETURN_HIGH)
    edge = lax.broadcasted_iota(jnp.int32, (tokens, BINS), 1).astype(jnp.float32) * width
    edge = edge + RETURN_LOW
    below = 0.5 * (1.0 + lax.erf((edge - returns) / scale))
    above = 0.5 * (1.0 + lax.erf((edge + width - returns) / scale))
    return (above - below) / (above[:, BINS - 1 :] - below[:, :1])


def forward_kernel(
    gain_exp, hidden, head, gain, rewards, old_values, mask, row_exp, pack, hidden_v, head_v, sems
):
    tokens, width = hidden.shape
    span = width // CHUNKS
    copies = []
    for n in range(CHUNKS):
        copies.append(
            pltpu.make_async_copy(
                hidden.at[:, n * span : (n + 1) * span], hidden_v.at[n], sems.at[n]
            )
        )
    for n in range(CHUNKS):
        copies.append(
            pltpu.make_async_copy(
                head.at[n * span : (n + 1) * span, :], head_v.at[n], sems.at[CHUNKS + n]
            )
        )
    for copy in copies:
        copy.start()
    blocks = width // LANES
    for n in range(blocks):
        pack[2 * tokens + n : 2 * tokens + n + 1, :] = limit_of(
            row_exp[:, n * LANES : (n + 1) * LANES]
        )
        pack[2 * tokens + blocks + n : 2 * tokens + blocks + n + 1, :] = limit_of(
            jnp.full((1, LANES), gain_exp[0, n], jnp.int32)
        )
    targets = target_mass(rewards[...], old_values[...], tokens)
    row = lax.broadcasted_iota(jnp.int32, (tokens, tokens), 0)
    column = lax.broadcasted_iota(jnp.int32, (tokens, tokens), 1)
    counted = jnp.where(row == column, mask[...].astype(jnp.float32), 0.0)
    counted = jnp.sum(counted, axis=1, keepdims=True)
    square = jnp.zeros((tokens, LANES), jnp.float32)
    for n in range(CHUNKS):
        copies[n].wait()
        part = hidden_v[n].astype(jnp.float32)
        part = part * part
        for m in range(span // LANES):
            square = square + part[:, m * LANES : (m + 1) * LANES]
    inv_rms = lax.rsqrt(jnp.sum(square, axis=1, keepdims=True) / width + NORM_EPSILON)
    gains = gain[...].astype(jnp.float32)
    logits = jnp.zeros((tokens, BINS), jnp.float32)
    for n in range(CHUNKS):
        copies[CHUNKS + n].wait()
        first = n * span // LANES
        gain_row = jnp.concatenate(
            [gains[first + m : first + m + 1, :] for m in range(span // LANES)], axis=1
        )
        normed = hidden_v[n].astype(jnp.float32) * inv_rms
        scaled = (normed * gain_row).astype(jnp.bfloat16)
        logits = logits + jnp.dot(scaled, head_v[n], preferred_element_type=jnp.float32)
    logits = LOGIT_SCALE * logits
    shifted = jnp.exp(logits - jnp.max(logits, axis=1, keepdims=True))
    probs = shifted / jnp.sum(shifted, axis=1, keepdims=True)
    errors = (LOGIT_SCALE * counted * (probs - targets)).astype(jnp.bfloat16)
    pack[:tokens, :] = errors.astype(jnp.float32)
    pack[tokens : 2 * tokens, :] = jnp.broadcast_to(inv_rms, (tokens, LANES))


def run_forward(hidden, head, gain, rewards, old_values, mask, row_exp, gain_exp):
    tokens, width = hidden.shape
    span = width // CHUNKS
    rows = 2 * tokens + 2 * (width // LANES)
    anywhere = pl.BlockSpec(memory_space=pl.ANY)
    vmem = pl.BlockSpec(memory_space=pltpu.VMEM)
    return pl.pallas_call(
        forward_kernel,
        out_shape=jax.ShapeDtypeStruct((rows, LANES), jnp.float32),
        in_specs=[pl.BlockSpec(memory_space=pltpu.SMEM), anywhere, anywhere] + [vmem] * 5,
        out_specs=vmem,
        scratch_shapes=[
            pltpu.VMEM((CHUNKS, tokens, span), jnp.bfloat16),
            pltpu.VMEM((CHUNKS, span, BINS), jnp.bfloat16),
            pltpu.SemaphoreType.DMA((2 * CHUNKS,)),
        ],
        cost_estimate=pl.CostEstimate(
            flops=2 * tokens * width * BINS, bytes_accessed=8 * width * tokens, transcendentals=0
        ),
        compiler_params=pltpu.CompilerParams(vmem_limit_bytes=63 * 2**20),
        name="forward",
    )(
        gain_exp,
        hidden,
        head,
        gain,
        rewards,
        old_values,
        mask,
        row_exp,
    )


def grads_kernel(
    place, hidden, other, head, gain, pack, other_pack, first_w, second_w, first_g, second_g,
    out, moments, hidden_v, head_v, gain_f, gain_sum, sems,
):
    tokens, width = hidden.shape
    size_z, span = head_v.shape[0], head_v.shape[1]
    tiles = span // LANES
    rows = span // out.shape[0]
    side = place[0]
    copies = []
    for z in range(size_z):
        start = pl.multiple_of((2 * z + side) * span, span)
        copies.append(
            (
                pltpu.make_async_copy(
                    hidden.at[:, pl.ds(start, span)], hidden_v.at[0, z], sems.at[0, z]
                ),
                pltpu.make_async_copy(
                    other.at[:, pl.ds(start, span)], hidden_v.at[1, z], sems.at[1, z]
                ),
                pltpu.make_async_copy(head.at[pl.ds(start, span), :], head_v.at[z], sems.at[2, z]),
            )
        )
        for copy in copies[-1]:
            copy.start()
    gain_f[...] = gain[...].astype(jnp.float32)
    owner = lax.broadcasted_iota(jnp.int32, (1, LANES), 1) // rows == place[1]
    moments[:rows, :] = first_w[...]
    moments[rows : 2 * rows, :] = second_w[...]
    for n, values in enumerate((first_g, second_g)):
        repeated = jnp.concatenate([values[...]] * (LANES // rows), axis=1)
        moments[2 * rows + n : 2 * rows + n + 1, :] = jnp.where(owner, repeated, 0.0)
    moments[2 * rows + 2 :, :] = jnp.zeros((6, LANES), jnp.float32)
    packs = (pack, other_pack)
    errors = [p[:tokens, :] for p in packs]
    flipped = [e.T.astype(jnp.bfloat16) for e in errors]
    errors = [e.astype(jnp.bfloat16) for e in errors]
    inv_rms = [jnp.concatenate([p[tokens : 2 * tokens, :]] * tiles, axis=1) for p in packs]
    blocks = width // LANES

    def spread(ref, first):
        return jnp.concatenate([ref[pl.ds(first + m, 1), :] for m in range(tiles)], axis=1)

    for z in range(size_z):
        for copy in copies[z]:
            copy.wait()
        first = (2 * z + side) * tiles
        gain_row = spread(gain_f, first)
        weight = jnp.zeros((BINS, span), jnp.float32)
        total = jnp.zeros((1, span), jnp.float32)
        for g in range(2):
            normed = hidden_v[g, z].astype(jnp.float32) * inv_rms[g]
            scaled = (normed * gain_row).astype(jnp.bfloat16)
            back = lax.dot_general(
                errors[g], head_v[z], (((1,), (1,)), ((), ())), preferred_element_type=jnp.float32
            )
            gain_part = jnp.sum(back * normed, axis=0, keepdims=True)
            limit = spread(packs[g], 2 * tokens + blocks + first)
            gain_q = jnp.clip(gain_part, -limit, limit).astype(jnp.bfloat16)
            total = total + gain_q.astype(jnp.float32)
            part = jnp.dot(flipped[g], scaled, preferred_element_type=jnp.float32)
            limit = spread(packs[g], 2 * tokens + first)
            weight_q = jnp.clip(part, -limit, limit).astype(jnp.bfloat16)
            weight = weight + weight_q.astype(jnp.float32)
        weight = weight.astype(jnp.bfloat16)
        for m in range(tiles):
            lanes = slice(m * LANES, (m + 1) * LANES)
            turned = weight[:, lanes].T
            gain_sum[m, z : z + 1, :] = total[:, lanes]
            for n in range(LANES // rows):
                out[m * (LANES // rows) + n, z * rows : (z + 1) * rows, :] = turned[
                    n * rows : (n + 1) * rows, :
                ]
    for m in range(tiles):
        high = gain_sum[m].astype(jnp.bfloat16)
        low = (gain_sum[m] - high.astype(jnp.float32)).astype(jnp.bfloat16)
        both = jnp.concatenate([high.astype(jnp.float32), low.astype(jnp.float32)], axis=0)
        for n in range(LANES // rows):
            out[m * (LANES // rows) + n, size_z * rows :, :] = both.astype(jnp.bfloat16)


def run_grads(place, hidden, other, head, gain, packs, moments, size_z, size_xy):
    tokens, width = hidden.shape
    span = width // (2 * size_z)
    rows = span // size_xy
    anywhere = pl.BlockSpec(memory_space=pl.ANY)
    vmem = pl.BlockSpec(memory_space=pltpu.VMEM)
    return pl.pallas_call(
        grads_kernel,
        out_shape=(
            jax.ShapeDtypeStruct((size_xy, size_z * rows + 2 * size_z, BINS), jnp.bfloat16),
            jax.ShapeDtypeStruct((2 * rows + 8, LANES), jnp.float32),
        ),
        in_specs=[pl.BlockSpec(memory_space=pltpu.SMEM), anywhere, anywhere, anywhere] + [vmem] * 7,
        out_specs=(vmem, vmem),
        scratch_shapes=[
            pltpu.VMEM((2, size_z, tokens, span), jnp.bfloat16),
            pltpu.VMEM((size_z, span, BINS), jnp.bfloat16),
            pltpu.VMEM((width // LANES, LANES), jnp.float32),
            pltpu.VMEM((span // LANES, size_z, LANES), jnp.float32),
            pltpu.SemaphoreType.DMA((3, size_z)),
        ],
        cost_estimate=pl.CostEstimate(
            flops=4 * tokens * width * BINS, bytes_accessed=8 * width * tokens, transcendentals=0
        ),
        compiler_params=pltpu.CompilerParams(vmem_limit_bytes=60 * 2**20),
        name="grads",
    )(place, hidden, other, head, gain, *packs, *moments)


def plane_kernel(parts, out):
    size_z = (parts.shape[1] - 2 * 8) // 32
    copies = out.shape[0] // size_z
    rows = 32
    total = parts[0].astype(jnp.float32)
    for n in range(1, parts.shape[0]):
        total = total + parts[n].astype(jnp.float32)
    for z in range(size_z):
        high_row = size_z * rows + z
        low_row = high_row + size_z
        gain = total[high_row : high_row + 1, :] + total[low_row : low_row + 1, :]
        high = gain.astype(jnp.bfloat16).astype(jnp.float32)
        block = jnp.concatenate(
            [
                total[z * rows : (z + 1) * rows, :],
                high,
                gain - high,
                jnp.zeros((6, LANES), jnp.float32),
            ],
            axis=0,
        ).astype(jnp.bfloat16)
        for n in range(copies):
            out[z * copies + n] = block


def run_plane(parts, size_z, size_pipe):
    vmem = pl.BlockSpec(memory_space=pltpu.VMEM)
    return pl.pallas_call(
        plane_kernel,
        out_shape=jax.ShapeDtypeStruct((size_z * size_pipe, 40, LANES), jnp.bfloat16),
        in_specs=[vmem],
        out_specs=vmem,
        compiler_params=pltpu.CompilerParams(vmem_limit_bytes=12 * 2**20),
        name="plane",
    )(parts)


def adam(param, grad, first, second):
    first_new = 0.9 * first + 0.1 * grad
    second_new = 0.95 * second + 0.05 * grad * grad
    update = first_new / FIRST_CORR / (jnp.sqrt(second_new / SECOND_CORR) + EPSILON)
    return param - LEARN_RATE * update, first_new, second_new


def update_kernel(
    place, parts, head, gain, own, next_1, next_2, next_3,
    new_weight, new_gain, first_w, second_w, first_g, second_g, weight_v, gain_f, sem,
):
    rows = first_w.shape[0]
    peers = LANES // rows
    size_z = parts.shape[0] // peers
    start = pl.multiple_of(place[2] * LANES, LANES)
    copy = pltpu.make_async_copy(head.at[pl.ds(start, LANES), :], weight_v, sem)
    copy.start()
    gain_f[...] = gain[...].astype(jnp.float32)
    moments = (own, next_1, next_2, next_3)
    grad = jnp.zeros((1, LANES), jnp.float32)
    for z in range(size_z):
        block = parts[z * peers].astype(jnp.float32)
        grad = grad + (block[rows : rows + 1, :] + block[rows + 1 : rows + 2, :])
    first, second = (
        sum(m[2 * rows + n : 2 * rows + n + 1, :] for m in moments[1:])
        + moments[0][2 * rows + n : 2 * rows + n + 1, :]
        for n in range(2)
    )
    updated, first, second = adam(gain_f[pl.ds(place[2], 1), :], grad, first, second)
    new_gain[...] = updated.astype(jnp.bfloat16)
    for ref, values in ((first_g, first), (second_g, second)):
        mine = jnp.zeros((1, rows), jnp.float32)
        for n in range(peers):
            mine = jnp.where(place[1] == n, values[:, n * rows : (n + 1) * rows], mine)
        ref[...] = mine
    copy.wait()
    for n in range(peers):
        peer = lax.rem(place[1] + n, peers)
        grad = jnp.zeros((rows, BINS), jnp.float32)
        for z in range(size_z):
            grad = grad + parts[z * peers + peer].astype(jnp.float32)[:rows, :]
        at = pl.multiple_of(peer * rows, rows)
        updated, first, second = adam(
            weight_v[pl.ds(at, rows), :].astype(jnp.float32),
            grad,
            moments[n][:rows, :],
            moments[n][rows : 2 * rows, :],
        )
        new_weight[pl.ds(at, rows), :] = updated.astype(jnp.bfloat16)
        if n == 0:
            first_w[...] = first
            second_w[...] = second


def run_update(place, parts, head, gain, moments):
    vmem = pl.BlockSpec(memory_space=pltpu.VMEM)
    rows = (moments[0].shape[0] - 8) // 2
    wide = jax.ShapeDtypeStruct((rows, BINS), jnp.float32)
    thin = jax.ShapeDtypeStruct((1, rows), jnp.float32)
    return pl.pallas_call(
        update_kernel,
        out_shape=(
            jax.ShapeDtypeStruct((LANES, BINS), jnp.bfloat16),
            jax.ShapeDtypeStruct((1, LANES), jnp.bfloat16),
            wide,
            wide,
            thin,
            thin,
        ),
        in_specs=[
            pl.BlockSpec(memory_space=pltpu.SMEM),
            vmem,
            pl.BlockSpec(memory_space=pl.ANY),
        ]
        + [vmem] * 5,
        out_specs=(vmem,) * 6,
        scratch_shapes=[
            pltpu.VMEM((LANES, BINS), jnp.bfloat16),
            pltpu.VMEM(gain.shape, jnp.float32),
            pltpu.SemaphoreType.DMA,
        ],
        compiler_params=pltpu.CompilerParams(vmem_limit_bytes=12 * 2**20),
        name="update",
    )(place, parts, head, gain, *moments)


def shards(
    final_hidden,
    value_head,
    norm_gain,
    rewards,
    old_values,
    loss_mask,
    row_exp,
    gain_exp,
    first_w,
    second_w,
    first_g,
    second_g,
):
    size_dp = lax.axis_size("dp")
    size_node = lax.axis_size("node")
    size_pipe = lax.axis_size("pipe")
    size_z = size_dp // 2
    size_xy = size_node * size_pipe
    rows = first_g.shape[0]
    tokens = final_hidden.shape[0]
    blocks = value_head.shape[0] // LANES
    dp, node, pipe = (lax.axis_index(name) for name in ("dp", "node", "pipe"))
    place = jnp.stack([lax.rem(dp, 2), pipe, dp * size_node + node]).astype(jnp.int32)
    swap = [(i, i ^ 1) for i in range(size_dp)]
    columns = [
        [((2 * z + c) * size_node + x) * size_pipe + y for z in range(size_z) for y in range(size_pipe)]
        for c in range(2)
        for x in range(size_node)
    ]

    other_hidden = lax.ppermute(final_hidden, "dp", swap)
    gain_blocks = norm_gain.reshape(blocks, LANES)
    pack = run_forward(
        final_hidden,
        value_head,
        gain_blocks,
        rewards.reshape(1, tokens),
        old_values.reshape(1, tokens),
        loss_mask.reshape(1, tokens),
        row_exp,
        gain_exp,
    )
    other_pack = lax.ppermute(pack, "dp", swap)
    packed, moments = run_grads(
        place,
        final_hidden,
        other_hidden,
        value_head,
        gain_blocks,
        (pack, other_pack),
        (first_w, second_w, first_g.reshape(1, rows), second_g.reshape(1, rows)),
        size_z,
        size_xy,
    )
    packed = lax.all_to_all(packed, ("node", "pipe"), 0, 0, tiled=True)
    moments = [moments] + [
        lax.ppermute(moments, "pipe", [(i, (i - k) % size_pipe) for i in range(size_pipe)])
        for k in range(1, size_pipe)
    ]
    packed = run_plane(packed, size_z, size_pipe)
    packed = lax.all_to_all(
        packed, ("dp", "node", "pipe"), 0, 0, tiled=True, axis_index_groups=columns
    )
    new_weight, new_gain, first_w, second_w, first_g, second_g = run_update(
        place, packed, value_head, gain_blocks, moments
    )
    return (
        new_weight,
        new_gain.reshape(size_pipe * rows),
        first_w,
        second_w,
        first_g.reshape(rows),
        second_g.reshape(rows),
    )


def solution(mesh):
    return jax.shard_map(
        shards,
        mesh=mesh,
        in_specs=(
            P(("dp", "node", "pipe"), None),
            P(),
            P(),
            P(("dp", "node", "pipe")),
            P(("dp", "node", "pipe")),
            P(("dp", "node", "pipe")),
            P(("dp", "node", "pipe"), None),
            P(("dp", "node", "pipe"), None),
            P(("dp", "node", "pipe"), None),
            P(("dp", "node", "pipe"), None),
            P(("dp", "node", "pipe")),
            P(("dp", "node", "pipe")),
        ),
        out_specs=(
            P(("dp", "node"), None),
            P(("dp", "node")),
            P(("dp", "node", "pipe"), None),
            P(("dp", "node", "pipe"), None),
            P(("dp", "node", "pipe")),
            P(("dp", "node", "pipe")),
        ),
        check_vma=False,
    )
```

```python
import math

import jax
import jax.numpy as jnp
from jax import lax
from jax.experimental import pallas as pl
from jax.experimental.pallas import tpu as pltpu
from jax.sharding import PartitionSpec as P

BINS = 128
GBLK = 128
SEQ = 32


LOGIT_SCALE = 0.0625
RETURN_LOW = -4.0
RETURN_HIGH = 4.0
TRACE_DECAY = 0.95
SAT_LIMIT = 448.0
LEARN_RATE = 0.02
FIRST_CORR = 0.19
SECOND_CORR = 0.0975
EPSILON = 1e-08
NORM_EPSILON = 1e-06


LANES = 128
CHUNKS = 4
LIMIT_BASE = 16


def limit_of(exponent):
    power = jnp.left_shift(jnp.ones_like(exponent), exponent + LIMIT_BASE)
    return power.astype(jnp.float32) * (SAT_LIMIT * 2.0**-LIMIT_BASE)


def target_mass(rewards, old_values, tokens):
    width = (RETURN_HIGH - RETURN_LOW) / BINS
    scale = 0.75 * width * math.sqrt(2.0)
    token = lax.broadcasted_iota(jnp.int32, (tokens, tokens), 0)
    later = lax.broadcasted_iota(jnp.int32, (tokens, tokens), 1)
    values = jnp.broadcast_to(old_values, (tokens, tokens))
    following = jnp.where(lax.rem(later, SEQ) == SEQ - 1, 0.0, pltpu.roll(values, tokens - 1, 1))
    td_error = rewards + following - values
    behind = (later - token).astype(jnp.float32)
    inside = jnp.logical_and(later >= token, lax.div(later, SEQ) == lax.div(token, SEQ))
    decay = jnp.where(inside, jnp.exp(jnp.maximum(behind, 0.0) * math.log(TRACE_DECAY)), 0.0)
    own = jnp.where(later == token, values, 0.0)
    returns = jnp.sum(decay * td_error + own, axis=1, keepdims=True)
    returns = jnp.clip(returns, RETURN_LOW, RETURN_HIGH)
    edge = lax.broadcasted_iota(jnp.int32, (tokens, BINS), 1).astype(jnp.float32) * width
    edge = edge + RETURN_LOW
    below = 0.5 * (1.0 + lax.erf((edge - returns) / scale))
    above = 0.5 * (1.0 + lax.erf((edge + width - returns) / scale))
    return (above - below) / (above[:, BINS - 1 :] - below[:, :1])


def forward_kernel(
    gain_exp, hidden, head, gain, rewards, old_values, mask, row_exp, pack, hidden_v, head_v, scaled_v, sems
):
    tokens, width = hidden.shape
    span = width // CHUNKS
    copies = []
    for n in range(CHUNKS):
        copies.append(
            pltpu.make_async_copy(
                hidden.at[:, n * span : (n + 1) * span], hidden_v.at[n], sems.at[n]
            )
        )
    for n in range(CHUNKS):
        copies.append(
            pltpu.make_async_copy(
                head.at[n * span : (n + 1) * span, :], head_v.at[n], sems.at[CHUNKS + n]
            )
        )
    for copy in copies:
        copy.start()
    blocks = width // LANES
    for n in range(blocks):
        pack[2 * tokens + n : 2 * tokens + n + 1, :] = limit_of(
            row_exp[:, n * LANES : (n + 1) * LANES]
        )
        pack[2 * tokens + blocks + n : 2 * tokens + blocks + n + 1, :] = limit_of(
            jnp.full((1, LANES), gain_exp[0, n], jnp.int32)
        )
    targets = target_mass(rewards[...], old_values[...], tokens)
    row = lax.broadcasted_iota(jnp.int32, (tokens, tokens), 0)
    column = lax.broadcasted_iota(jnp.int32, (tokens, tokens), 1)
    counted = jnp.where(row == column, mask[...].astype(jnp.float32), 0.0)
    counted = jnp.sum(counted, axis=1, keepdims=True)
    square = jnp.zeros((tokens, LANES), jnp.float32)
    for n in range(CHUNKS):
        copies[n].wait()
        for m in range(span // LANES):
            part = hidden_v[n, :, m * LANES : (m + 1) * LANES].astype(jnp.float32)
            square = square + part * part
    inv_rms = lax.rsqrt(jnp.sum(square, axis=1, keepdims=True) / width + NORM_EPSILON)
    gains = gain[...].astype(jnp.float32)
    for n in range(CHUNKS):
        first = n * span // LANES
        for m in range(span // LANES):
            normed = hidden_v[n, :, m * LANES : (m + 1) * LANES].astype(jnp.float32) * inv_rms
            at = n * span + m * LANES
            scaled_v[:, at : at + LANES] = (normed * gains[first + m : first + m + 1, :]).astype(
                jnp.bfloat16
            )
    for n in range(CHUNKS):
        copies[CHUNKS + n].wait()
    logits = LOGIT_SCALE * jnp.dot(
        scaled_v[...], head_v[...].reshape(width, BINS), preferred_element_type=jnp.float32
    )
    shifted = jnp.exp(logits - jnp.max(logits, axis=1, keepdims=True))
    probs = shifted / jnp.sum(shifted, axis=1, keepdims=True)
    errors = (LOGIT_SCALE * counted * (probs - targets)).astype(jnp.bfloat16)
    pack[:tokens, :] = errors.astype(jnp.float32)
    pack[tokens : 2 * tokens, :] = jnp.broadcast_to(inv_rms, (tokens, LANES))


def run_forward(hidden, head, gain, rewards, old_values, mask, row_exp, gain_exp):
    tokens, width = hidden.shape
    span = width // CHUNKS
    rows = 2 * tokens + 2 * (width // LANES)
    anywhere = pl.BlockSpec(memory_space=pl.ANY)
    vmem = pl.BlockSpec(memory_space=pltpu.VMEM)
    return pl.pallas_call(
        forward_kernel,
        out_shape=jax.ShapeDtypeStruct((rows, LANES), jnp.float32),
        in_specs=[pl.BlockSpec(memory_space=pltpu.SMEM), anywhere, anywhere] + [vmem] * 5,
        out_specs=vmem,
        scratch_shapes=[
            pltpu.VMEM((CHUNKS, tokens, span), jnp.bfloat16),
            pltpu.VMEM((CHUNKS, span, BINS), jnp.bfloat16),
            pltpu.VMEM((tokens, width), jnp.bfloat16),
            pltpu.SemaphoreType.DMA((2 * CHUNKS,)),
        ],
        cost_estimate=pl.CostEstimate(
            flops=2 * tokens * width * BINS, bytes_accessed=8 * width * tokens, transcendentals=0
        ),
        compiler_params=pltpu.CompilerParams(vmem_limit_bytes=63 * 2**20),
        name="forward",
    )(
        gain_exp,
        hidden,
        head,
        gain,
        rewards,
        old_values,
        mask,
        row_exp,
    )


def grads_kernel(
    place, hidden, other, head, gain, pack, other_pack, first_w, second_w, first_g, second_g,
    out, moments, hidden_v, head_v, gain_f, gain_sum, sems,
):
    tokens, width = hidden.shape
    size_z, span = head_v.shape[0], head_v.shape[1]
    tiles = span // LANES
    rows = span // out.shape[0]
    side = place[0]
    copies = []
    for z in range(size_z):
        start = pl.multiple_of((2 * z + side) * span, span)
        copies.append(
            (
                pltpu.make_async_copy(
                    hidden.at[:, pl.ds(start, span)], hidden_v.at[0, z], sems.at[0, z]
                ),
                pltpu.make_async_copy(
                    other.at[:, pl.ds(start, span)], hidden_v.at[1, z], sems.at[1, z]
                ),
                pltpu.make_async_copy(head.at[pl.ds(start, span), :], head_v.at[z], sems.at[2, z]),
            )
        )
        for copy in copies[-1]:
            copy.start()
    gain_f[...] = gain[...].astype(jnp.float32)
    owner = lax.broadcasted_iota(jnp.int32, (1, LANES), 1) // rows == place[1]
    moments[:rows, :] = first_w[...]
    moments[rows : 2 * rows, :] = second_w[...]
    for n, values in enumerate((first_g, second_g)):
        repeated = jnp.concatenate([values[...]] * (LANES // rows), axis=1)
        moments[2 * rows + n : 2 * rows + n + 1, :] = jnp.where(owner, repeated, 0.0)
    moments[2 * rows + 2 :, :] = jnp.zeros((6, LANES), jnp.float32)
    packs = (pack, other_pack)
    errors = [p[:tokens, :] for p in packs]
    flipped = [e.T.astype(jnp.bfloat16) for e in errors]
    errors = [e.astype(jnp.bfloat16) for e in errors]
    piece = 256
    inv_rms = [jnp.concatenate([p[tokens : 2 * tokens, :]] * (piece // LANES), axis=1) for p in packs]
    blocks = width // LANES

    def spread(ref, first):
        return jnp.concatenate(
            [ref[pl.ds(first + m, 1), :] for m in range(piece // LANES)], axis=1
        )

    for z in range(size_z):
        for copy in copies[z]:
            copy.wait()
        for s in range(span // piece):
            lanes = slice(s * piece, (s + 1) * piece)
            first = (2 * z + side) * tiles + s * (piece // LANES)
            gain_row = spread(gain_f, first)
            weight = jnp.zeros((BINS, piece), jnp.float32)
            total = jnp.zeros((1, piece), jnp.float32)
            for g in range(2):
                back = lax.dot_general(
                    errors[g],
                    head_v[z, lanes, :],
                    (((1,), (1,)), ((), ())),
                    preferred_element_type=jnp.float32,
                )
                normed = hidden_v[g, z, :, lanes].astype(jnp.float32) * inv_rms[g]
                scaled = (normed * gain_row).astype(jnp.bfloat16)
                part = jnp.dot(flipped[g], scaled, preferred_element_type=jnp.float32)
                gain_part = jnp.sum(back * normed, axis=0, keepdims=True)
                limit = spread(packs[g], 2 * tokens + blocks + first)
                gain_q = jnp.clip(gain_part, -limit, limit).astype(jnp.bfloat16)
                total = total + gain_q.astype(jnp.float32)
                limit = spread(packs[g], 2 * tokens + first)
                weight_q = jnp.clip(part, -limit, limit).astype(jnp.bfloat16)
                weight = weight + weight_q.astype(jnp.float32)
            weight = weight.astype(jnp.bfloat16)
            for m in range(piece // LANES):
                turned = weight[:, m * LANES : (m + 1) * LANES].T
                tile = s * (piece // LANES) + m
                gain_sum[tile, z : z + 1, :] = total[:, m * LANES : (m + 1) * LANES]
                for n in range(LANES // rows):
                    out[tile * (LANES // rows) + n, z * rows : (z + 1) * rows, :] = turned[
                        n * rows : (n + 1) * rows, :
                    ]
    for m in range(tiles):
        high = gain_sum[m].astype(jnp.bfloat16)
        low = (gain_sum[m] - high.astype(jnp.float32)).astype(jnp.bfloat16)
        both = jnp.concatenate([high.astype(jnp.float32), low.astype(jnp.float32)], axis=0)
        for n in range(LANES // rows):
            out[m * (LANES // rows) + n, size_z * rows :, :] = both.astype(jnp.bfloat16)


def run_grads(place, hidden, other, head, gain, packs, moments, size_z, size_xy):
    tokens, width = hidden.shape
    span = width // (2 * size_z)
    rows = span // size_xy
    anywhere = pl.BlockSpec(memory_space=pl.ANY)
    vmem = pl.BlockSpec(memory_space=pltpu.VMEM)
    return pl.pallas_call(
        grads_kernel,
        out_shape=(
            jax.ShapeDtypeStruct((size_xy, size_z * rows + 2 * size_z, BINS), jnp.bfloat16),
            jax.ShapeDtypeStruct((2 * rows + 8, LANES), jnp.float32),
        ),
        in_specs=[pl.BlockSpec(memory_space=pltpu.SMEM), anywhere, anywhere, anywhere] + [vmem] * 7,
        out_specs=(vmem, vmem),
        scratch_shapes=[
            pltpu.VMEM((2, size_z, tokens, span), jnp.bfloat16),
            pltpu.VMEM((size_z, span, BINS), jnp.bfloat16),
            pltpu.VMEM((width // LANES, LANES), jnp.float32),
            pltpu.VMEM((span // LANES, size_z, LANES), jnp.float32),
            pltpu.SemaphoreType.DMA((3, size_z)),
        ],
        cost_estimate=pl.CostEstimate(
            flops=4 * tokens * width * BINS, bytes_accessed=8 * width * tokens, transcendentals=0
        ),
        compiler_params=pltpu.CompilerParams(vmem_limit_bytes=54579 * 2**10),
        name="grads",
    )(place, hidden, other, head, gain, *packs, *moments)


def plane_kernel(parts, out):
    size_z = (parts.shape[1] - 2 * 8) // 32
    copies = out.shape[0] // size_z
    rows = 32
    total = parts[0].astype(jnp.float32)
    for n in range(1, parts.shape[0]):
        total = total + parts[n].astype(jnp.float32)
    for z in range(size_z):
        high_row = size_z * rows + z
        low_row = high_row + size_z
        gain = total[high_row : high_row + 1, :] + total[low_row : low_row + 1, :]
        high = gain.astype(jnp.bfloat16).astype(jnp.float32)
        block = jnp.concatenate(
            [
                total[z * rows : (z + 1) * rows, :],
                high,
                gain - high,
                jnp.zeros((6, LANES), jnp.float32),
            ],
            axis=0,
        ).astype(jnp.bfloat16)
        for n in range(copies):
            out[z * copies + n] = block


def run_plane(parts, size_z, size_pipe):
    vmem = pl.BlockSpec(memory_space=pltpu.VMEM)
    return pl.pallas_call(
        plane_kernel,
        out_shape=jax.ShapeDtypeStruct((size_z * size_pipe, 40, LANES), jnp.bfloat16),
        in_specs=[vmem],
        out_specs=vmem,
        compiler_params=pltpu.CompilerParams(vmem_limit_bytes=12 * 2**20),
        name="plane",
    )(parts)


def adam(param, grad, first, second):
    first_new = 0.9 * first + 0.1 * grad
    second_new = 0.95 * second + 0.05 * grad * grad
    update = first_new / FIRST_CORR / (jnp.sqrt(second_new / SECOND_CORR) + EPSILON)
    return param - LEARN_RATE * update, first_new, second_new


def update_kernel(
    place, parts, head, gain, own, next_1, next_2, next_3,
    new_weight, new_gain, first_w, second_w, first_g, second_g, weight_v, gain_f, sem,
):
    rows = first_w.shape[0]
    peers = LANES // rows
    size_z = parts.shape[0] // peers
    start = pl.multiple_of(place[2] * LANES, LANES)
    copy = pltpu.make_async_copy(head.at[pl.ds(start, LANES), :], weight_v, sem)
    copy.start()
    gain_f[...] = gain[...].astype(jnp.float32)
    moments = (own, next_1, next_2, next_3)
    grad = jnp.zeros((1, LANES), jnp.float32)
    for z in range(size_z):
        block = parts[z * peers].astype(jnp.float32)
        grad = grad + (block[rows : rows + 1, :] + block[rows + 1 : rows + 2, :])
    first, second = (
        sum(m[2 * rows + n : 2 * rows + n + 1, :] for m in moments[1:])
        + moments[0][2 * rows + n : 2 * rows + n + 1, :]
        for n in range(2)
    )
    updated, first, second = adam(gain_f[pl.ds(place[2], 1), :], grad, first, second)
    new_gain[...] = updated.astype(jnp.bfloat16)
    for ref, values in ((first_g, first), (second_g, second)):
        mine = jnp.zeros((1, rows), jnp.float32)
        for n in range(peers):
            mine = jnp.where(place[1] == n, values[:, n * rows : (n + 1) * rows], mine)
        ref[...] = mine
    copy.wait()
    for n in range(peers):
        peer = lax.rem(place[1] + n, peers)
        grad = jnp.zeros((rows, BINS), jnp.float32)
        for z in range(size_z):
            grad = grad + parts[z * peers + peer].astype(jnp.float32)[:rows, :]
        at = pl.multiple_of(peer * rows, rows)
        updated, first, second = adam(
            weight_v[pl.ds(at, rows), :].astype(jnp.float32),
            grad,
            moments[n][:rows, :],
            moments[n][rows : 2 * rows, :],
        )
        new_weight[pl.ds(at, rows), :] = updated.astype(jnp.bfloat16)
        if n == 0:
            first_w[...] = first
            second_w[...] = second


def run_update(place, parts, head, gain, moments):
    vmem = pl.BlockSpec(memory_space=pltpu.VMEM)
    rows = (moments[0].shape[0] - 8) // 2
    wide = jax.ShapeDtypeStruct((rows, BINS), jnp.float32)
    thin = jax.ShapeDtypeStruct((1, rows), jnp.float32)
    return pl.pallas_call(
        update_kernel,
        out_shape=(
            jax.ShapeDtypeStruct((LANES, BINS), jnp.bfloat16),
            jax.ShapeDtypeStruct((1, LANES), jnp.bfloat16),
            wide,
            wide,
            thin,
            thin,
        ),
        in_specs=[
            pl.BlockSpec(memory_space=pltpu.SMEM),
            vmem,
            pl.BlockSpec(memory_space=pl.ANY),
        ]
        + [vmem] * 5,
        out_specs=(vmem,) * 6,
        scratch_shapes=[
            pltpu.VMEM((LANES, BINS), jnp.bfloat16),
            pltpu.VMEM(gain.shape, jnp.float32),
            pltpu.SemaphoreType.DMA,
        ],
        compiler_params=pltpu.CompilerParams(vmem_limit_bytes=12 * 2**20),
        name="update",
    )(place, parts, head, gain, *moments)


def shards(
    final_hidden,
    value_head,
    norm_gain,
    rewards,
    old_values,
    loss_mask,
    row_exp,
    gain_exp,
    first_w,
    second_w,
    first_g,
    second_g,
):
    size_dp = lax.axis_size("dp")
    size_node = lax.axis_size("node")
    size_pipe = lax.axis_size("pipe")
    size_z = size_dp // 2
    size_xy = size_node * size_pipe
    rows = first_g.shape[0]
    tokens = final_hidden.shape[0]
    blocks = value_head.shape[0] // LANES
    dp, node, pipe = (lax.axis_index(name) for name in ("dp", "node", "pipe"))
    place = jnp.stack([lax.rem(dp, 2), pipe, dp * size_node + node]).astype(jnp.int32)
    swap = [(i, i ^ 1) for i in range(size_dp)]
    columns = [
        [((2 * z + c) * size_node + x) * size_pipe + y for z in range(size_z) for y in range(size_pipe)]
        for c in range(2)
        for x in range(size_node)
    ]

    other_hidden = lax.ppermute(final_hidden, "dp", swap)
    gain_blocks = norm_gain.reshape(blocks, LANES)
    pack = run_forward(
        final_hidden,
        value_head,
        gain_blocks,
        rewards.reshape(1, tokens),
        old_values.reshape(1, tokens),
        loss_mask.reshape(1, tokens),
        row_exp,
        gain_exp,
    )
    other_pack = lax.ppermute(pack, "dp", swap)
    packed, moments = run_grads(
        place,
        final_hidden,
        other_hidden,
        value_head,
        gain_blocks,
        (pack, other_pack),
        (first_w, second_w, first_g.reshape(1, rows), second_g.reshape(1, rows)),
        size_z,
        size_xy,
    )
    packed = lax.all_to_all(packed, ("node", "pipe"), 0, 0, tiled=True)
    moments = [moments] + [
        lax.ppermute(moments, "pipe", [(i, (i - k) % size_pipe) for i in range(size_pipe)])
        for k in range(1, size_pipe)
    ]
    packed = run_plane(packed, size_z, size_pipe)
    packed = lax.all_to_all(
        packed, ("dp", "node", "pipe"), 0, 0, tiled=True, axis_index_groups=columns
    )
    new_weight, new_gain, first_w, second_w, first_g, second_g = run_update(
        place, packed, value_head, gain_blocks, moments
    )
    return (
        new_weight,
        new_gain.reshape(size_pipe * rows),
        first_w,
        second_w,
        first_g.reshape(rows),
        second_g.reshape(rows),
    )


def solution(mesh):
    return jax.shard_map(
        shards,
        mesh=mesh,
        in_specs=(
            P(("dp", "node", "pipe"), None),
            P(),
            P(),
            P(("dp", "node", "pipe")),
            P(("dp", "node", "pipe")),
            P(("dp", "node", "pipe")),
            P(("dp", "node", "pipe"), None),
            P(("dp", "node", "pipe"), None),
            P(("dp", "node", "pipe"), None),
            P(("dp", "node", "pipe"), None),
            P(("dp", "node", "pipe")),
            P(("dp", "node", "pipe")),
        ),
        out_specs=(
            P(("dp", "node"), None),
            P(("dp", "node")),
            P(("dp", "node", "pipe"), None),
            P(("dp", "node", "pipe"), None),
            P(("dp", "node", "pipe")),
            P(("dp", "node", "pipe")),
        ),
        check_vma=False,
    )
```

```python
import math

import jax
import jax.numpy as jnp
from jax import lax
from jax.experimental import pallas as pl
from jax.experimental.pallas import tpu as pltpu
from jax.sharding import PartitionSpec as P

BINS = 128
GBLK = 128
SEQ = 32


LOGIT_SCALE = 0.0625
RETURN_LOW = -4.0
RETURN_HIGH = 4.0
TRACE_DECAY = 0.95
SAT_LIMIT = 448.0
LEARN_RATE = 0.02
FIRST_CORR = 0.19
SECOND_CORR = 0.0975
EPSILON = 1e-08
NORM_EPSILON = 1e-06


LANES = 128
CHUNKS = 4
LIMIT_BASE = 16


def limit_of(exponent):
    power = jnp.left_shift(jnp.ones_like(exponent), exponent + LIMIT_BASE)
    return power.astype(jnp.float32) * (SAT_LIMIT * 2.0**-LIMIT_BASE)


def target_mass(rewards, old_values, tokens):
    width = (RETURN_HIGH - RETURN_LOW) / BINS
    scale = 0.75 * width * math.sqrt(2.0)
    token = lax.broadcasted_iota(jnp.int32, (tokens, tokens), 0)
    later = lax.broadcasted_iota(jnp.int32, (tokens, tokens), 1)
    values = jnp.broadcast_to(old_values, (tokens, tokens))
    following = jnp.where(lax.rem(later, SEQ) == SEQ - 1, 0.0, pltpu.roll(values, tokens - 1, 1))
    td_error = rewards + following - values
    behind = (later - token).astype(jnp.float32)
    inside = jnp.logical_and(later >= token, lax.div(later, SEQ) == lax.div(token, SEQ))
    decay = jnp.where(inside, jnp.exp(jnp.maximum(behind, 0.0) * math.log(TRACE_DECAY)), 0.0)
    own = jnp.where(later == token, values, 0.0)
    returns = jnp.sum(decay * td_error + own, axis=1, keepdims=True)
    returns = jnp.clip(returns, RETURN_LOW, RETURN_HIGH)
    edge = lax.broadcasted_iota(jnp.int32, (tokens, BINS), 1).astype(jnp.float32) * width
    edge = edge + RETURN_LOW
    below = 0.5 * (1.0 + lax.erf((edge - returns) / scale))
    above = 0.5 * (1.0 + lax.erf((edge + width - returns) / scale))
    return (above - below) / (above[:, BINS - 1 :] - below[:, :1])


def forward_kernel(
    gain_exp, hidden, head, gain, rewards, old_values, mask, row_exp, pack, hidden_v, head_v, scaled_v, sems
):
    tokens, width = hidden.shape
    span = width // CHUNKS
    copies = []
    for n in range(CHUNKS):
        copies.append(
            pltpu.make_async_copy(
                hidden.at[:, n * span : (n + 1) * span], hidden_v.at[n], sems.at[n]
            )
        )
    for n in range(CHUNKS):
        copies.append(
            pltpu.make_async_copy(
                head.at[n * span : (n + 1) * span, :], head_v.at[n], sems.at[CHUNKS + n]
            )
        )
    for copy in copies:
        copy.start()
    blocks = width // LANES
    for n in range(blocks):
        pack[2 * tokens + n : 2 * tokens + n + 1, :] = limit_of(
            row_exp[:, n * LANES : (n + 1) * LANES]
        )
        pack[2 * tokens + blocks + n : 2 * tokens + blocks + n + 1, :] = limit_of(
            jnp.full((1, LANES), gain_exp[0, n], jnp.int32)
        )
    targets = target_mass(rewards[...], old_values[...], tokens)
    row = lax.broadcasted_iota(jnp.int32, (tokens, tokens), 0)
    column = lax.broadcasted_iota(jnp.int32, (tokens, tokens), 1)
    counted = jnp.where(row == column, mask[...].astype(jnp.float32), 0.0)
    counted = jnp.sum(counted, axis=1, keepdims=True)
    square = jnp.zeros((tokens, LANES), jnp.float32)
    for n in range(CHUNKS):
        copies[n].wait()
        for m in range(span // LANES):
            part = hidden_v[n, :, m * LANES : (m + 1) * LANES].astype(jnp.float32)
            square = square + part * part
    inv_rms = lax.rsqrt(jnp.sum(square, axis=1, keepdims=True) / width + NORM_EPSILON)
    gains = gain[...].astype(jnp.float32)
    for n in range(CHUNKS):
        first = n * span // LANES
        for m in range(span // LANES):
            normed = hidden_v[n, :, m * LANES : (m + 1) * LANES].astype(jnp.float32) * inv_rms
            at = n * span + m * LANES
            scaled_v[:, at : at + LANES] = (normed * gains[first + m : first + m + 1, :]).astype(
                jnp.bfloat16
            )
    for n in range(CHUNKS):
        copies[CHUNKS + n].wait()
    logits = LOGIT_SCALE * jnp.dot(
        scaled_v[...], head_v[...].reshape(width, BINS), preferred_element_type=jnp.float32
    )
    shifted = jnp.exp(logits - jnp.max(logits, axis=1, keepdims=True))
    probs = shifted / jnp.sum(shifted, axis=1, keepdims=True)
    errors = (LOGIT_SCALE * counted * (probs - targets)).astype(jnp.bfloat16)
    pack[:tokens, :] = errors.astype(jnp.float32)
    pack[tokens : 2 * tokens, :] = jnp.broadcast_to(inv_rms, (tokens, LANES))


def run_forward(hidden, head, gain, rewards, old_values, mask, row_exp, gain_exp):
    tokens, width = hidden.shape
    span = width // CHUNKS
    rows = 2 * tokens + 2 * (width // LANES)
    anywhere = pl.BlockSpec(memory_space=pl.ANY)
    vmem = pl.BlockSpec(memory_space=pltpu.VMEM)
    return pl.pallas_call(
        forward_kernel,
        out_shape=jax.ShapeDtypeStruct((rows, LANES), jnp.float32),
        in_specs=[pl.BlockSpec(memory_space=pltpu.SMEM), anywhere, anywhere] + [vmem] * 5,
        out_specs=vmem,
        scratch_shapes=[
            pltpu.VMEM((CHUNKS, tokens, span), jnp.bfloat16),
            pltpu.VMEM((CHUNKS, span, BINS), jnp.bfloat16),
            pltpu.VMEM((tokens, width), jnp.bfloat16),
            pltpu.SemaphoreType.DMA((2 * CHUNKS,)),
        ],
        cost_estimate=pl.CostEstimate(
            flops=2 * tokens * width * BINS, bytes_accessed=8 * width * tokens, transcendentals=0
        ),
        compiler_params=pltpu.CompilerParams(vmem_limit_bytes=63 * 2**20),
        name="forward",
    )(
        gain_exp,
        hidden,
        head,
        gain,
        rewards,
        old_values,
        mask,
        row_exp,
    )


def grads_kernel(
    place, hidden, other, head, gain, pack, other_pack, first_w, second_w, first_g, second_g,
    out, moments, hidden_v, head_v, gain_f, gain_sum, sems,
):
    tokens, width = hidden.shape
    size_z, span = head_v.shape[0], head_v.shape[1]
    tiles = span // LANES
    rows = span // out.shape[0]
    side = place[0]
    copies = []
    for z in range(size_z):
        start = pl.multiple_of((2 * z + side) * span, span)
        copies.append(
            (
                pltpu.make_async_copy(
                    hidden.at[:, pl.ds(start, span)], hidden_v.at[0, z], sems.at[0, z]
                ),
                pltpu.make_async_copy(
                    other.at[:, pl.ds(start, span)], hidden_v.at[1, z], sems.at[1, z]
                ),
                pltpu.make_async_copy(head.at[pl.ds(start, span), :], head_v.at[z], sems.at[2, z]),
            )
        )
        for copy in copies[-1]:
            copy.start()
    gain_f[...] = gain[...].astype(jnp.float32)
    owner = lax.broadcasted_iota(jnp.int32, (1, LANES), 1) // rows == place[1]
    moments[:rows, :] = first_w[...]
    moments[rows : 2 * rows, :] = second_w[...]
    for n, values in enumerate((first_g, second_g)):
        repeated = jnp.concatenate([values[...]] * (LANES // rows), axis=1)
        moments[2 * rows + n : 2 * rows + n + 1, :] = jnp.where(owner, repeated, 0.0)
    moments[2 * rows + 2 :, :] = jnp.zeros((6, LANES), jnp.float32)
    packs = (pack, other_pack)
    errors = [p[:tokens, :] for p in packs]
    flipped = [e.T.astype(jnp.bfloat16) for e in errors]
    errors = [e.astype(jnp.bfloat16) for e in errors]
    piece = 256
    inv_rms = [jnp.concatenate([p[tokens : 2 * tokens, :]] * (piece // LANES), axis=1) for p in packs]
    blocks = width // LANES

    def spread(ref, first):
        return jnp.concatenate(
            [ref[pl.ds(first + m, 1), :] for m in range(piece // LANES)], axis=1
        )

    for z in range(size_z):
        for copy in copies[z]:
            copy.wait()
        for s in range(span // piece):
            lanes = slice(s * piece, (s + 1) * piece)
            first = (2 * z + side) * tiles + s * (piece // LANES)
            gain_row = spread(gain_f, first)
            weight = jnp.zeros((BINS, piece), jnp.float32)
            total = jnp.zeros((1, piece), jnp.float32)
            for g in range(2):
                back = lax.dot_general(
                    errors[g],
                    head_v[z, lanes, :],
                    (((1,), (1,)), ((), ())),
                    preferred_element_type=jnp.float32,
                )
                normed = hidden_v[g, z, :, lanes].astype(jnp.float32) * inv_rms[g]
                scaled = (normed * gain_row).astype(jnp.bfloat16)
                part = jnp.dot(flipped[g], scaled, preferred_element_type=jnp.float32)
                gain_part = jnp.sum(back * normed, axis=0, keepdims=True)
                limit = spread(packs[g], 2 * tokens + blocks + first)
                gain_q = jnp.clip(gain_part, -limit, limit).astype(jnp.bfloat16)
                total = total + gain_q.astype(jnp.float32)
                limit = spread(packs[g], 2 * tokens + first)
                weight_q = jnp.clip(part, -limit, limit).astype(jnp.bfloat16)
                weight = weight + weight_q.astype(jnp.float32)
            weight = weight.astype(jnp.bfloat16)
            for m in range(piece // LANES):
                turned = weight[:, m * LANES : (m + 1) * LANES].T
                tile = s * (piece // LANES) + m
                gain_sum[tile, z : z + 1, :] = total[:, m * LANES : (m + 1) * LANES]
                for n in range(LANES // rows):
                    out[tile * (LANES // rows) + n, z * rows : (z + 1) * rows, :] = turned[
                        n * rows : (n + 1) * rows, :
                    ]
    for m in range(tiles):
        high = gain_sum[m].astype(jnp.bfloat16)
        low = (gain_sum[m] - high.astype(jnp.float32)).astype(jnp.bfloat16)
        both = jnp.concatenate([high.astype(jnp.float32), low.astype(jnp.float32)], axis=0)
        for n in range(LANES // rows):
            out[m * (LANES // rows) + n, size_z * rows :, :] = both.astype(jnp.bfloat16)


def run_grads(place, hidden, other, head, gain, packs, moments, size_z, size_xy):
    tokens, width = hidden.shape
    span = width // (2 * size_z)
    rows = span // size_xy
    anywhere = pl.BlockSpec(memory_space=pl.ANY)
    vmem = pl.BlockSpec(memory_space=pltpu.VMEM)
    return pl.pallas_call(
        grads_kernel,
        out_shape=(
            jax.ShapeDtypeStruct((size_xy, size_z * rows + 2 * size_z, BINS), jnp.bfloat16),
            jax.ShapeDtypeStruct((2 * rows + 8, LANES), jnp.float32),
        ),
        in_specs=[pl.BlockSpec(memory_space=pltpu.SMEM), anywhere, anywhere, anywhere] + [vmem] * 7,
        out_specs=(vmem, vmem),
        scratch_shapes=[
            pltpu.VMEM((2, size_z, tokens, span), jnp.bfloat16),
            pltpu.VMEM((size_z, span, BINS), jnp.bfloat16),
            pltpu.VMEM((width // LANES, LANES), jnp.float32),
            pltpu.VMEM((span // LANES, size_z, LANES), jnp.float32),
            pltpu.SemaphoreType.DMA((3, size_z)),
        ],
        cost_estimate=pl.CostEstimate(
            flops=4 * tokens * width * BINS, bytes_accessed=8 * width * tokens, transcendentals=0
        ),
        compiler_params=pltpu.CompilerParams(vmem_limit_bytes=53248 * 2**10),
        name="grads",
    )(place, hidden, other, head, gain, *packs, *moments)


def plane_kernel(parts, out):
    size_z = (parts.shape[1] - 2 * 8) // 32
    copies = out.shape[0] // size_z
    rows = 32
    total = parts[0].astype(jnp.float32)
    for n in range(1, parts.shape[0]):
        total = total + parts[n].astype(jnp.float32)
    for z in range(size_z):
        high_row = size_z * rows + z
        low_row = high_row + size_z
        gain = total[high_row : high_row + 1, :] + total[low_row : low_row + 1, :]
        high = gain.astype(jnp.bfloat16).astype(jnp.float32)
        block = jnp.concatenate(
            [
                total[z * rows : (z + 1) * rows, :],
                high,
                gain - high,
                jnp.zeros((6, LANES), jnp.float32),
            ],
            axis=0,
        ).astype(jnp.bfloat16)
        for n in range(copies):
            out[z * copies + n] = block


def run_plane(parts, size_z, size_pipe):
    vmem = pl.BlockSpec(memory_space=pltpu.VMEM)
    return pl.pallas_call(
        plane_kernel,
        out_shape=jax.ShapeDtypeStruct((size_z * size_pipe, 40, LANES), jnp.bfloat16),
        in_specs=[vmem],
        out_specs=vmem,
        compiler_params=pltpu.CompilerParams(vmem_limit_bytes=12 * 2**20),
        name="plane",
    )(parts)


def adam(param, grad, first, second):
    first_new = 0.9 * first + 0.1 * grad
    second_new = 0.95 * second + 0.05 * grad * grad
    update = first_new / FIRST_CORR / (jnp.sqrt(second_new / SECOND_CORR) + EPSILON)
    return param - LEARN_RATE * update, first_new, second_new


def update_kernel(
    place, parts, head, gain, own, next_1, next_2, next_3,
    new_weight, new_gain, first_w, second_w, first_g, second_g, weight_v, gain_f, sem,
):
    rows = first_w.shape[0]
    peers = LANES // rows
    size_z = parts.shape[0] // peers
    start = pl.multiple_of(place[2] * LANES, LANES)
    copy = pltpu.make_async_copy(head.at[pl.ds(start, LANES), :], weight_v, sem)
    copy.start()
    gain_f[...] = gain[...].astype(jnp.float32)
    moments = (own, next_1, next_2, next_3)
    grad = jnp.zeros((1, LANES), jnp.float32)
    for z in range(size_z):
        block = parts[z * peers].astype(jnp.float32)
        grad = grad + (block[rows : rows + 1, :] + block[rows + 1 : rows + 2, :])
    first, second = (
        sum(m[2 * rows + n : 2 * rows + n + 1, :] for m in moments[1:])
        + moments[0][2 * rows + n : 2 * rows + n + 1, :]
        for n in range(2)
    )
    updated, first, second = adam(gain_f[pl.ds(place[2], 1), :], grad, first, second)
    new_gain[...] = updated.astype(jnp.bfloat16)
    for ref, values in ((first_g, first), (second_g, second)):
        mine = jnp.zeros((1, rows), jnp.float32)
        for n in range(peers):
            mine = jnp.where(place[1] == n, values[:, n * rows : (n + 1) * rows], mine)
        ref[...] = mine
    copy.wait()
    for n in range(peers):
        peer = lax.rem(place[1] + n, peers)
        grad = jnp.zeros((rows, BINS), jnp.float32)
        for z in range(size_z):
            grad = grad + parts[z * peers + peer].astype(jnp.float32)[:rows, :]
        at = pl.multiple_of(peer * rows, rows)
        updated, first, second = adam(
            weight_v[pl.ds(at, rows), :].astype(jnp.float32),
            grad,
            moments[n][:rows, :],
            moments[n][rows : 2 * rows, :],
        )
        new_weight[pl.ds(at, rows), :] = updated.astype(jnp.bfloat16)
        if n == 0:
            first_w[...] = first
            second_w[...] = second


def run_update(place, parts, head, gain, moments):
    vmem = pl.BlockSpec(memory_space=pltpu.VMEM)
    rows = (moments[0].shape[0] - 8) // 2
    wide = jax.ShapeDtypeStruct((rows, BINS), jnp.float32)
    thin = jax.ShapeDtypeStruct((1, rows), jnp.float32)
    return pl.pallas_call(
        update_kernel,
        out_shape=(
            jax.ShapeDtypeStruct((LANES, BINS), jnp.bfloat16),
            jax.ShapeDtypeStruct((1, LANES), jnp.bfloat16),
            wide,
            wide,
            thin,
            thin,
        ),
        in_specs=[
            pl.BlockSpec(memory_space=pltpu.SMEM),
            vmem,
            pl.BlockSpec(memory_space=pl.ANY),
        ]
        + [vmem] * 5,
        out_specs=(vmem,) * 6,
        scratch_shapes=[
            pltpu.VMEM((LANES, BINS), jnp.bfloat16),
            pltpu.VMEM(gain.shape, jnp.float32),
            pltpu.SemaphoreType.DMA,
        ],
        compiler_params=pltpu.CompilerParams(vmem_limit_bytes=12 * 2**20),
        name="update",
    )(place, parts, head, gain, *moments)


def shards(
    final_hidden,
    value_head,
    norm_gain,
    rewards,
    old_values,
    loss_mask,
    row_exp,
    gain_exp,
    first_w,
    second_w,
    first_g,
    second_g,
):
    size_dp = lax.axis_size("dp")
    size_node = lax.axis_size("node")
    size_pipe = lax.axis_size("pipe")
    size_z = size_dp // 2
    size_xy = size_node * size_pipe
    rows = first_g.shape[0]
    tokens = final_hidden.shape[0]
    blocks = value_head.shape[0] // LANES
    dp, node, pipe = (lax.axis_index(name) for name in ("dp", "node", "pipe"))
    place = jnp.stack([lax.rem(dp, 2), pipe, dp * size_node + node]).astype(jnp.int32)
    swap = [(i, i ^ 1) for i in range(size_dp)]
    columns = [
        [((2 * z + c) * size_node + x) * size_pipe + y for z in range(size_z) for y in range(size_pipe)]
        for c in range(2)
        for x in range(size_node)
    ]

    other_hidden = lax.ppermute(final_hidden, "dp", swap)
    gain_blocks = norm_gain.reshape(blocks, LANES)
    pack = run_forward(
        final_hidden,
        value_head,
        gain_blocks,
        rewards.reshape(1, tokens),
        old_values.reshape(1, tokens),
        loss_mask.reshape(1, tokens),
        row_exp,
        gain_exp,
    )
    other_pack = lax.ppermute(pack, "dp", swap)
    packed, moments = run_grads(
        place,
        final_hidden,
        other_hidden,
        value_head,
        gain_blocks,
        (pack, other_pack),
        (first_w, second_w, first_g.reshape(1, rows), second_g.reshape(1, rows)),
        size_z,
        size_xy,
    )
    packed = lax.all_to_all(packed, ("node", "pipe"), 0, 0, tiled=True)
    moments = [moments] + [
        lax.ppermute(moments, "pipe", [(i, (i - k) % size_pipe) for i in range(size_pipe)])
        for k in range(1, size_pipe)
    ]
    packed = run_plane(packed, size_z, size_pipe)
    packed = lax.all_to_all(
        packed, ("dp", "node", "pipe"), 0, 0, tiled=True, axis_index_groups=columns
    )
    new_weight, new_gain, first_w, second_w, first_g, second_g = run_update(
        place, packed, value_head, gain_blocks, moments
    )
    return (
        new_weight,
        new_gain.reshape(size_pipe * rows),
        first_w,
        second_w,
        first_g.reshape(rows),
        second_g.reshape(rows),
    )


def solution(mesh):
    return jax.shard_map(
        shards,
        mesh=mesh,
        in_specs=(
            P(("dp", "node", "pipe"), None),
            P(),
            P(),
            P(("dp", "node", "pipe")),
            P(("dp", "node", "pipe")),
            P(("dp", "node", "pipe")),
            P(("dp", "node", "pipe"), None),
            P(("dp", "node", "pipe"), None),
            P(("dp", "node", "pipe"), None),
            P(("dp", "node", "pipe"), None),
            P(("dp", "node", "pipe")),
            P(("dp", "node", "pipe")),
        ),
        out_specs=(
            P(("dp", "node"), None),
            P(("dp", "node")),
            P(("dp", "node", "pipe"), None),
            P(("dp", "node", "pipe"), None),
            P(("dp", "node", "pipe")),
            P(("dp", "node", "pipe")),
        ),
        check_vma=False,
    )
```

```python
import math

import jax
import jax.numpy as jnp
from jax import lax
from jax.experimental import pallas as pl
from jax.experimental.pallas import tpu as pltpu
from jax.sharding import PartitionSpec as P

BINS = 128
GBLK = 128
SEQ = 32


LOGIT_SCALE = 0.0625
RETURN_LOW = -4.0
RETURN_HIGH = 4.0
TRACE_DECAY = 0.95
SAT_LIMIT = 448.0
LEARN_RATE = 0.02
FIRST_CORR = 0.19
SECOND_CORR = 0.0975
EPSILON = 1e-08
NORM_EPSILON = 1e-06


LANES = 128
CHUNKS = 4
LIMIT_BASE = 16
KEPT_ROWS = 24576


def limit_of(exponent):
    power = jnp.left_shift(jnp.ones_like(exponent), exponent + LIMIT_BASE)
    return power.astype(jnp.float32) * (SAT_LIMIT * 2.0**-LIMIT_BASE)


def target_mass(rewards, old_values, tokens):
    width = (RETURN_HIGH - RETURN_LOW) / BINS
    scale = 0.75 * width * math.sqrt(2.0)
    token = lax.broadcasted_iota(jnp.int32, (tokens, tokens), 0)
    later = lax.broadcasted_iota(jnp.int32, (tokens, tokens), 1)
    values = jnp.broadcast_to(old_values, (tokens, tokens))
    following = jnp.where(lax.rem(later, SEQ) == SEQ - 1, 0.0, pltpu.roll(values, tokens - 1, 1))
    td_error = rewards + following - values
    behind = (later - token).astype(jnp.float32)
    inside = jnp.logical_and(later >= token, lax.div(later, SEQ) == lax.div(token, SEQ))
    decay = jnp.where(inside, jnp.exp(jnp.maximum(behind, 0.0) * math.log(TRACE_DECAY)), 0.0)
    own = jnp.where(later == token, values, 0.0)
    returns = jnp.sum(decay * td_error + own, axis=1, keepdims=True)
    returns = jnp.clip(returns, RETURN_LOW, RETURN_HIGH)
    edge = lax.broadcasted_iota(jnp.int32, (tokens, BINS), 1).astype(jnp.float32) * width
    edge = edge + RETURN_LOW
    below = 0.5 * (1.0 + lax.erf((edge - returns) / scale))
    above = 0.5 * (1.0 + lax.erf((edge + width - returns) / scale))
    return (above - below) / (above[:, BINS - 1 :] - below[:, :1])


def forward_kernel(
    gain_exp, hidden, head, gain, rewards, old_values, mask, row_exp, sent, kept,
    pack, hidden_v, head_v, scaled_v, sems, out_sems,
):
    tokens, width = hidden.shape
    span = width // CHUNKS
    copies = []
    for n in range(CHUNKS):
        copies.append(
            pltpu.make_async_copy(
                hidden.at[:, n * span : (n + 1) * span], hidden_v.at[n], sems.at[n]
            )
        )
    for n in range(CHUNKS):
        copies.append(
            pltpu.make_async_copy(
                head.at[n * span : (n + 1) * span, :], head_v.at[n], sems.at[CHUNKS + n]
            )
        )
    for copy in copies:
        copy.start()
    blocks = width // LANES
    for n in range(blocks):
        pack[2 * tokens + n : 2 * tokens + n + 1, :] = limit_of(
            row_exp[:, n * LANES : (n + 1) * LANES]
        )
        pack[2 * tokens + blocks + n : 2 * tokens + blocks + n + 1, :] = limit_of(
            jnp.full((1, LANES), gain_exp[0, n], jnp.int32)
        )
    targets = target_mass(rewards[...], old_values[...], tokens)
    row = lax.broadcasted_iota(jnp.int32, (tokens, tokens), 0)
    column = lax.broadcasted_iota(jnp.int32, (tokens, tokens), 1)
    counted = jnp.where(row == column, mask[...].astype(jnp.float32), 0.0)
    counted = jnp.sum(counted, axis=1, keepdims=True)
    square = jnp.zeros((tokens, LANES), jnp.float32)
    for n in range(CHUNKS):
        copies[n].wait()
        for m in range(span // LANES):
            part = hidden_v[n, :, m * LANES : (m + 1) * LANES].astype(jnp.float32)
            square = square + part * part
    inv_rms = lax.rsqrt(jnp.sum(square, axis=1, keepdims=True) / width + NORM_EPSILON)
    gains = gain[...].astype(jnp.float32)
    for n in range(CHUNKS):
        first = n * span // LANES
        for m in range(span // LANES):
            normed = hidden_v[n, :, m * LANES : (m + 1) * LANES].astype(jnp.float32) * inv_rms
            at = n * span + m * LANES
            scaled_v[:, at : at + LANES] = (normed * gains[first + m : first + m + 1, :]).astype(
                jnp.bfloat16
            )
    for n in range(CHUNKS):
        copies[CHUNKS + n].wait()
    logits = LOGIT_SCALE * jnp.dot(
        scaled_v[...], head_v[...].reshape(width, BINS), preferred_element_type=jnp.float32
    )
    shifted = jnp.exp(logits - jnp.max(logits, axis=1, keepdims=True))
    probs = shifted / jnp.sum(shifted, axis=1, keepdims=True)
    errors = (LOGIT_SCALE * counted * (probs - targets)).astype(jnp.bfloat16)
    pack[:tokens, :] = errors.astype(jnp.float32)
    pack[tokens : 2 * tokens, :] = jnp.broadcast_to(inv_rms, (tokens, LANES))
    rows = pack.shape[0]
    results = [
        pltpu.make_async_copy(pack, sent, out_sems.at[0]),
        pltpu.make_async_copy(pack, kept.at[:rows, :], out_sems.at[1]),
    ]
    for copy in results:
        copy.start()
    for copy in results:
        copy.wait()


def run_forward(hidden, head, gain, rewards, old_values, mask, row_exp, gain_exp):
    tokens, width = hidden.shape
    span = width // CHUNKS
    rows = 2 * tokens + 2 * (width // LANES)
    anywhere = pl.BlockSpec(memory_space=pl.ANY)
    vmem = pl.BlockSpec(memory_space=pltpu.VMEM)
    return pl.pallas_call(
        forward_kernel,
        out_shape=(
            jax.ShapeDtypeStruct((rows, LANES), jnp.float32),
            jax.ShapeDtypeStruct((KEPT_ROWS, LANES), jnp.float32),
        ),
        in_specs=[pl.BlockSpec(memory_space=pltpu.SMEM), anywhere, anywhere] + [vmem] * 5,
        out_specs=(anywhere, anywhere),
        scratch_shapes=[
            pltpu.VMEM((rows, LANES), jnp.float32),
            pltpu.VMEM((CHUNKS, tokens, span), jnp.bfloat16),
            pltpu.VMEM((CHUNKS, span, BINS), jnp.bfloat16),
            pltpu.VMEM((tokens, width), jnp.bfloat16),
            pltpu.SemaphoreType.DMA((2 * CHUNKS,)),
            pltpu.SemaphoreType.DMA((2,)),
        ],
        cost_estimate=pl.CostEstimate(
            flops=2 * tokens * width * BINS, bytes_accessed=8 * width * tokens, transcendentals=0
        ),
        compiler_params=pltpu.CompilerParams(vmem_limit_bytes=63 * 2**20),
        name="forward",
    )(
        gain_exp,
        hidden,
        head,
        gain,
        rewards,
        old_values,
        mask,
        row_exp,
    )


def grads_kernel(
    place, hidden, other, head, kept, gain, other_pack, first_w, second_w, first_g, second_g,
    out, moments, hidden_v, head_v, gain_f, gain_sum, pack, sems, kept_sem,
):
    tokens, width = hidden.shape
    size_z, span = head_v.shape[0], head_v.shape[1]
    tiles = span // LANES
    rows = span // out.shape[0]
    side = place[0]
    own = pltpu.make_async_copy(kept.at[: pack.shape[0], :], pack, kept_sem)
    own.start()
    copies = []
    for z in range(size_z):
        start = pl.multiple_of((2 * z + side) * span, span)
        copies.append(
            (
                pltpu.make_async_copy(
                    hidden.at[:, pl.ds(start, span)], hidden_v.at[0, z], sems.at[0, z]
                ),
                pltpu.make_async_copy(
                    other.at[:, pl.ds(start, span)], hidden_v.at[1, z], sems.at[1, z]
                ),
                pltpu.make_async_copy(head.at[pl.ds(start, span), :], head_v.at[z], sems.at[2, z]),
            )
        )
        for copy in copies[-1]:
            copy.start()
    gain_f[...] = gain[...].astype(jnp.float32)
    owner = lax.broadcasted_iota(jnp.int32, (1, LANES), 1) // rows == place[1]
    moments[:rows, :] = first_w[...]
    moments[rows : 2 * rows, :] = second_w[...]
    for n, values in enumerate((first_g, second_g)):
        repeated = jnp.concatenate([values[...]] * (LANES // rows), axis=1)
        moments[2 * rows + n : 2 * rows + n + 1, :] = jnp.where(owner, repeated, 0.0)
    moments[2 * rows + 2 :, :] = jnp.zeros((6, LANES), jnp.float32)
    own.wait()
    packs = (pack, other_pack)
    errors = [p[:tokens, :] for p in packs]
    flipped = [e.T.astype(jnp.bfloat16) for e in errors]
    errors = [e.astype(jnp.bfloat16) for e in errors]
    piece = 256
    inv_rms = [jnp.concatenate([p[tokens : 2 * tokens, :]] * (piece // LANES), axis=1) for p in packs]
    blocks = width // LANES

    def spread(ref, first):
        return jnp.concatenate(
            [ref[pl.ds(first + m, 1), :] for m in range(piece // LANES)], axis=1
        )

    for z in range(size_z):
        for copy in copies[z]:
            copy.wait()
        for s in range(span // piece):
            lanes = slice(s * piece, (s + 1) * piece)
            first = (2 * z + side) * tiles + s * (piece // LANES)
            gain_row = spread(gain_f, first)
            weight = jnp.zeros((BINS, piece), jnp.float32)
            total = jnp.zeros((1, piece), jnp.float32)
            for g in range(2):
                back = lax.dot_general(
                    errors[g],
                    head_v[z, lanes, :],
                    (((1,), (1,)), ((), ())),
                    preferred_element_type=jnp.float32,
                )
                normed = hidden_v[g, z, :, lanes].astype(jnp.float32) * inv_rms[g]
                scaled = (normed * gain_row).astype(jnp.bfloat16)
                part = jnp.dot(flipped[g], scaled, preferred_element_type=jnp.float32)
                gain_part = jnp.sum(back * normed, axis=0, keepdims=True)
                limit = spread(packs[g], 2 * tokens + blocks + first)
                gain_q = jnp.clip(gain_part, -limit, limit).astype(jnp.bfloat16)
                total = total + gain_q.astype(jnp.float32)
                limit = spread(packs[g], 2 * tokens + first)
                weight_q = jnp.clip(part, -limit, limit).astype(jnp.bfloat16)
                weight = weight + weight_q.astype(jnp.float32)
            weight = weight.astype(jnp.bfloat16)
            for m in range(piece // LANES):
                turned = weight[:, m * LANES : (m + 1) * LANES].T
                tile = s * (piece // LANES) + m
                gain_sum[tile, z : z + 1, :] = total[:, m * LANES : (m + 1) * LANES]
                for n in range(LANES // rows):
                    out[tile * (LANES // rows) + n, z * rows : (z + 1) * rows, :] = turned[
                        n * rows : (n + 1) * rows, :
                    ]
    for m in range(tiles):
        high = gain_sum[m].astype(jnp.bfloat16)
        low = (gain_sum[m] - high.astype(jnp.float32)).astype(jnp.bfloat16)
        both = jnp.concatenate([high.astype(jnp.float32), low.astype(jnp.float32)], axis=0)
        for n in range(LANES // rows):
            out[m * (LANES // rows) + n, size_z * rows :, :] = both.astype(jnp.bfloat16)


def run_grads(place, hidden, other, head, gain, packs, moments, size_z, size_xy):
    tokens, width = hidden.shape
    span = width // (2 * size_z)
    rows = span // size_xy
    anywhere = pl.BlockSpec(memory_space=pl.ANY)
    vmem = pl.BlockSpec(memory_space=pltpu.VMEM)
    return pl.pallas_call(
        grads_kernel,
        out_shape=(
            jax.ShapeDtypeStruct((size_xy, size_z * rows + 2 * size_z, BINS), jnp.bfloat16),
            jax.ShapeDtypeStruct((2 * rows + 8, LANES), jnp.float32),
        ),
        in_specs=[pl.BlockSpec(memory_space=pltpu.SMEM)] + [anywhere] * 4 + [vmem] * 6,
        out_specs=(vmem, vmem),
        scratch_shapes=[
            pltpu.VMEM((2, size_z, tokens, span), jnp.bfloat16),
            pltpu.VMEM((size_z, span, BINS), jnp.bfloat16),
            pltpu.VMEM((width // LANES, LANES), jnp.float32),
            pltpu.VMEM((span // LANES, size_z, LANES), jnp.float32),
            pltpu.VMEM(packs[1].shape, jnp.float32),
            pltpu.SemaphoreType.DMA((3, size_z)),
            pltpu.SemaphoreType.DMA,
        ],
        cost_estimate=pl.CostEstimate(
            flops=4 * tokens * width * BINS, bytes_accessed=8 * width * tokens, transcendentals=0
        ),
        compiler_params=pltpu.CompilerParams(vmem_limit_bytes=53248 * 2**10),
        name="grads",
    )(place, hidden, other, head, packs[0], gain, packs[1], *moments)


def plane_kernel(parts, out):
    size_z = (parts.shape[1] - 2 * 8) // 32
    copies = out.shape[0] // size_z
    rows = 32
    total = parts[0].astype(jnp.float32)
    for n in range(1, parts.shape[0]):
        total = total + parts[n].astype(jnp.float32)
    for z in range(size_z):
        high_row = size_z * rows + z
        low_row = high_row + size_z
        gain = total[high_row : high_row + 1, :] + total[low_row : low_row + 1, :]
        high = gain.astype(jnp.bfloat16).astype(jnp.float32)
        block = jnp.concatenate(
            [
                total[z * rows : (z + 1) * rows, :],
                high,
                gain - high,
                jnp.zeros((6, LANES), jnp.float32),
            ],
            axis=0,
        ).astype(jnp.bfloat16)
        for n in range(copies):
            out[z * copies + n] = block


def run_plane(parts, size_z, size_pipe):
    vmem = pl.BlockSpec(memory_space=pltpu.VMEM)
    return pl.pallas_call(
        plane_kernel,
        out_shape=jax.ShapeDtypeStruct((size_z * size_pipe, 40, LANES), jnp.bfloat16),
        in_specs=[vmem],
        out_specs=vmem,
        compiler_params=pltpu.CompilerParams(vmem_limit_bytes=12 * 2**20),
        name="plane",
    )(parts)


def adam(param, grad, first, second):
    first_new = 0.9 * first + 0.1 * grad
    second_new = 0.95 * second + 0.05 * grad * grad
    update = first_new / FIRST_CORR / (jnp.sqrt(second_new / SECOND_CORR) + EPSILON)
    return param - LEARN_RATE * update, first_new, second_new


def update_kernel(
    place, parts, head, gain, own, next_1, next_2, next_3,
    new_weight, new_gain, first_w, second_w, first_g, second_g, weight_v, gain_f, sem,
):
    rows = first_w.shape[0]
    peers = LANES // rows
    size_z = parts.shape[0] // peers
    start = pl.multiple_of(place[2] * LANES, LANES)
    copy = pltpu.make_async_copy(head.at[pl.ds(start, LANES), :], weight_v, sem)
    copy.start()
    gain_f[...] = gain[...].astype(jnp.float32)
    moments = (own, next_1, next_2, next_3)
    grad = jnp.zeros((1, LANES), jnp.float32)
    for z in range(size_z):
        block = parts[z * peers].astype(jnp.float32)
        grad = grad + (block[rows : rows + 1, :] + block[rows + 1 : rows + 2, :])
    first, second = (
        sum(m[2 * rows + n : 2 * rows + n + 1, :] for m in moments[1:])
        + moments[0][2 * rows + n : 2 * rows + n + 1, :]
        for n in range(2)
    )
    updated, first, second = adam(gain_f[pl.ds(place[2], 1), :], grad, first, second)
    new_gain[...] = updated.astype(jnp.bfloat16)
    for ref, values in ((first_g, first), (second_g, second)):
        mine = jnp.zeros((1, rows), jnp.float32)
        for n in range(peers):
            mine = jnp.where(place[1] == n, values[:, n * rows : (n + 1) * rows], mine)
        ref[...] = mine
    copy.wait()
    for n in range(peers):
        peer = lax.rem(place[1] + n, peers)
        grad = jnp.zeros((rows, BINS), jnp.float32)
        for z in range(size_z):
            grad = grad + parts[z * peers + peer].astype(jnp.float32)[:rows, :]
        at = pl.multiple_of(peer * rows, rows)
        updated, first, second = adam(
            weight_v[pl.ds(at, rows), :].astype(jnp.float32),
            grad,
            moments[n][:rows, :],
            moments[n][rows : 2 * rows, :],
        )
        new_weight[pl.ds(at, rows), :] = updated.astype(jnp.bfloat16)
        if n == 0:
            first_w[...] = first
            second_w[...] = second


def run_update(place, parts, head, gain, moments):
    vmem = pl.BlockSpec(memory_space=pltpu.VMEM)
    rows = (moments[0].shape[0] - 8) // 2
    wide = jax.ShapeDtypeStruct((rows, BINS), jnp.float32)
    thin = jax.ShapeDtypeStruct((1, rows), jnp.float32)
    return pl.pallas_call(
        update_kernel,
        out_shape=(
            jax.ShapeDtypeStruct((LANES, BINS), jnp.bfloat16),
            jax.ShapeDtypeStruct((1, LANES), jnp.bfloat16),
            wide,
            wide,
            thin,
            thin,
        ),
        in_specs=[
            pl.BlockSpec(memory_space=pltpu.SMEM),
            vmem,
            pl.BlockSpec(memory_space=pl.ANY),
        ]
        + [vmem] * 5,
        out_specs=(vmem,) * 6,
        scratch_shapes=[
            pltpu.VMEM((LANES, BINS), jnp.bfloat16),
            pltpu.VMEM(gain.shape, jnp.float32),
            pltpu.SemaphoreType.DMA,
        ],
        compiler_params=pltpu.CompilerParams(vmem_limit_bytes=12 * 2**20),
        name="update",
    )(place, parts, head, gain, *moments)


def shards(
    final_hidden,
    value_head,
    norm_gain,
    rewards,
    old_values,
    loss_mask,
    row_exp,
    gain_exp,
    first_w,
    second_w,
    first_g,
    second_g,
):
    size_dp = lax.axis_size("dp")
    size_node = lax.axis_size("node")
    size_pipe = lax.axis_size("pipe")
    size_z = size_dp // 2
    size_xy = size_node * size_pipe
    rows = first_g.shape[0]
    tokens = final_hidden.shape[0]
    blocks = value_head.shape[0] // LANES
    dp, node, pipe = (lax.axis_index(name) for name in ("dp", "node", "pipe"))
    place = jnp.stack([lax.rem(dp, 2), pipe, dp * size_node + node]).astype(jnp.int32)
    swap = [(i, i ^ 1) for i in range(size_dp)]
    columns = [
        [((2 * z + c) * size_node + x) * size_pipe + y for z in range(size_z) for y in range(size_pipe)]
        for c in range(2)
        for x in range(size_node)
    ]

    other_hidden = lax.ppermute(final_hidden, "dp", swap)
    gain_blocks = norm_gain.reshape(blocks, LANES)
    pack, kept = run_forward(
        final_hidden,
        value_head,
        gain_blocks,
        rewards.reshape(1, tokens),
        old_values.reshape(1, tokens),
        loss_mask.reshape(1, tokens),
        row_exp,
        gain_exp,
    )
    other_pack = lax.ppermute(pack, "dp", swap)
    packed, moments = run_grads(
        place,
        final_hidden,
        other_hidden,
        value_head,
        gain_blocks,
        (kept, other_pack),
        (first_w, second_w, first_g.reshape(1, rows), second_g.reshape(1, rows)),
        size_z,
        size_xy,
    )
    packed = lax.all_to_all(packed, ("node", "pipe"), 0, 0, tiled=True)
    moments = [moments] + [
        lax.ppermute(moments, "pipe", [(i, (i - k) % size_pipe) for i in range(size_pipe)])
        for k in range(1, size_pipe)
    ]
    packed = run_plane(packed, size_z, size_pipe)
    packed = lax.all_to_all(
        packed, ("dp", "node", "pipe"), 0, 0, tiled=True, axis_index_groups=columns
    )
    new_weight, new_gain, first_w, second_w, first_g, second_g = run_update(
        place, packed, value_head, gain_blocks, moments
    )
    return (
        new_weight,
        new_gain.reshape(size_pipe * rows),
        first_w,
        second_w,
        first_g.reshape(rows),
        second_g.reshape(rows),
    )


def solution(mesh):
    return jax.shard_map(
        shards,
        mesh=mesh,
        in_specs=(
            P(("dp", "node", "pipe"), None),
            P(),
            P(),
            P(("dp", "node", "pipe")),
            P(("dp", "node", "pipe")),
            P(("dp", "node", "pipe")),
            P(("dp", "node", "pipe"), None),
            P(("dp", "node", "pipe"), None),
            P(("dp", "node", "pipe"), None),
            P(("dp", "node", "pipe"), None),
            P(("dp", "node", "pipe")),
            P(("dp", "node", "pipe")),
        ),
        out_specs=(
            P(("dp", "node"), None),
            P(("dp", "node")),
            P(("dp", "node", "pipe"), None),
            P(("dp", "node", "pipe"), None),
            P(("dp", "node", "pipe")),
            P(("dp", "node", "pipe")),
        ),
        check_vma=False,
    )
```

```python
import math

import jax
import jax.numpy as jnp
from jax import lax
from jax.experimental import pallas as pl
from jax.experimental.pallas import tpu as pltpu
from jax.sharding import PartitionSpec as P

BINS = 128
GBLK = 128
SEQ = 32


LOGIT_SCALE = 0.0625
RETURN_LOW = -4.0
RETURN_HIGH = 4.0
TRACE_DECAY = 0.95
SAT_LIMIT = 448.0
LEARN_RATE = 0.02
FIRST_CORR = 0.19
SECOND_CORR = 0.0975
EPSILON = 1e-08
NORM_EPSILON = 1e-06


LANES = 128
CHUNKS = 4
LIMIT_BASE = 16
KEPT_ROWS = 24576


def limit_of(exponent):
    power = jnp.left_shift(jnp.ones_like(exponent), exponent + LIMIT_BASE)
    return power.astype(jnp.float32) * (SAT_LIMIT * 2.0**-LIMIT_BASE)


def target_mass(rewards, old_values, tokens):
    width = (RETURN_HIGH - RETURN_LOW) / BINS
    scale = 0.75 * width * math.sqrt(2.0)
    token = lax.broadcasted_iota(jnp.int32, (tokens, tokens), 0)
    later = lax.broadcasted_iota(jnp.int32, (tokens, tokens), 1)
    values = jnp.broadcast_to(old_values, (tokens, tokens))
    following = jnp.where(lax.rem(later, SEQ) == SEQ - 1, 0.0, pltpu.roll(values, tokens - 1, 1))
    td_error = rewards + following - values
    behind = (later - token).astype(jnp.float32)
    inside = jnp.logical_and(later >= token, lax.div(later, SEQ) == lax.div(token, SEQ))
    decay = jnp.where(inside, jnp.exp(jnp.maximum(behind, 0.0) * math.log(TRACE_DECAY)), 0.0)
    own = jnp.where(later == token, values, 0.0)
    returns = jnp.sum(decay * td_error + own, axis=1, keepdims=True)
    returns = jnp.clip(returns, RETURN_LOW, RETURN_HIGH)
    edge = lax.broadcasted_iota(jnp.int32, (tokens, BINS), 1).astype(jnp.float32) * width
    edge = edge + RETURN_LOW
    below = 0.5 * (1.0 + lax.erf((edge - returns) / scale))
    above = 0.5 * (1.0 + lax.erf((edge + width - returns) / scale))
    return (above - below) / (above[:, BINS - 1 :] - below[:, :1])


def forward_kernel(
    gain_exp, hidden, head, gain, rewards, old_values, mask, row_exp, sent, kept,
    pack, hidden_v, head_v, scaled_v, sems, out_sems,
):
    tokens, width = hidden.shape
    span = width // CHUNKS
    copies = []
    for n in range(CHUNKS):
        copies.append(
            pltpu.make_async_copy(
                hidden.at[:, n * span : (n + 1) * span], hidden_v.at[n], sems.at[n]
            )
        )
    for n in range(CHUNKS):
        copies.append(
            pltpu.make_async_copy(
                head.at[n * span : (n + 1) * span, :], head_v.at[n], sems.at[CHUNKS + n]
            )
        )
    for copy in copies:
        copy.start()
    blocks = width // LANES
    for n in range(blocks):
        pack[2 * tokens + n : 2 * tokens + n + 1, :] = limit_of(
            row_exp[:, n * LANES : (n + 1) * LANES]
        )
        pack[2 * tokens + blocks + n : 2 * tokens + blocks + n + 1, :] = limit_of(
            jnp.full((1, LANES), gain_exp[0, n], jnp.int32)
        )
    targets = target_mass(rewards[...], old_values[...], tokens)
    row = lax.broadcasted_iota(jnp.int32, (tokens, tokens), 0)
    column = lax.broadcasted_iota(jnp.int32, (tokens, tokens), 1)
    counted = jnp.where(row == column, mask[...].astype(jnp.float32), 0.0)
    counted = jnp.sum(counted, axis=1, keepdims=True)
    square = jnp.zeros((tokens, LANES), jnp.float32)
    for n in range(CHUNKS):
        copies[n].wait()
        for m in range(span // LANES):
            part = hidden_v[n, :, m * LANES : (m + 1) * LANES].astype(jnp.float32)
            square = square + part * part
    inv_rms = lax.rsqrt(jnp.sum(square, axis=1, keepdims=True) / width + NORM_EPSILON)
    gains = gain[...].astype(jnp.float32)
    for n in range(CHUNKS):
        first = n * span // LANES
        for m in range(span // LANES):
            normed = hidden_v[n, :, m * LANES : (m + 1) * LANES].astype(jnp.float32) * inv_rms
            at = n * span + m * LANES
            scaled_v[:, at : at + LANES] = (normed * gains[first + m : first + m + 1, :]).astype(
                jnp.bfloat16
            )
    for n in range(CHUNKS):
        copies[CHUNKS + n].wait()
    logits = LOGIT_SCALE * jnp.dot(
        scaled_v[...], head_v[...].reshape(width, BINS), preferred_element_type=jnp.float32
    )
    shifted = jnp.exp(logits - jnp.max(logits, axis=1, keepdims=True))
    probs = shifted / jnp.sum(shifted, axis=1, keepdims=True)
    errors = (LOGIT_SCALE * counted * (probs - targets)).astype(jnp.bfloat16)
    pack[:tokens, :] = errors.astype(jnp.float32)
    pack[tokens : 2 * tokens, :] = jnp.broadcast_to(inv_rms, (tokens, LANES))
    rows = pack.shape[0]
    results = [
        pltpu.make_async_copy(pack, sent, out_sems.at[0]),
        pltpu.make_async_copy(pack, kept.at[:rows, :], out_sems.at[1]),
    ]
    for copy in results:
        copy.start()
    for copy in results:
        copy.wait()


def run_forward(hidden, head, gain, rewards, old_values, mask, row_exp, gain_exp):
    tokens, width = hidden.shape
    span = width // CHUNKS
    rows = 2 * tokens + 2 * (width // LANES)
    anywhere = pl.BlockSpec(memory_space=pl.ANY)
    vmem = pl.BlockSpec(memory_space=pltpu.VMEM)
    return pl.pallas_call(
        forward_kernel,
        out_shape=(
            jax.ShapeDtypeStruct((rows, LANES), jnp.float32),
            jax.ShapeDtypeStruct((KEPT_ROWS, LANES), jnp.float32),
        ),
        in_specs=[pl.BlockSpec(memory_space=pltpu.SMEM), anywhere, anywhere] + [vmem] * 5,
        out_specs=(anywhere, anywhere),
        scratch_shapes=[
            pltpu.VMEM((rows, LANES), jnp.float32),
            pltpu.VMEM((CHUNKS, tokens, span), jnp.bfloat16),
            pltpu.VMEM((CHUNKS, span, BINS), jnp.bfloat16),
            pltpu.VMEM((tokens, width), jnp.bfloat16),
            pltpu.SemaphoreType.DMA((2 * CHUNKS,)),
            pltpu.SemaphoreType.DMA((2,)),
        ],
        cost_estimate=pl.CostEstimate(
            flops=2 * tokens * width * BINS, bytes_accessed=8 * width * tokens, transcendentals=0
        ),
        compiler_params=pltpu.CompilerParams(vmem_limit_bytes=63 * 2**20),
        name="forward",
    )(
        gain_exp,
        hidden,
        head,
        gain,
        rewards,
        old_values,
        mask,
        row_exp,
    )


def grads_kernel(
    place, hidden, other, head, kept, gain, other_pack, first_w, second_w, first_g, second_g,
    out, moments, hidden_v, head_v, gain_f, gain_sum, pack, sems, kept_sem,
):
    tokens, width = hidden.shape
    size_z, span = head_v.shape[0], head_v.shape[1]
    tiles = span // LANES
    rows = span // out.shape[0]
    side = place[0]
    own = pltpu.make_async_copy(kept.at[: pack.shape[0], :], pack, kept_sem)
    own.start()
    copies = []
    for z in range(size_z):
        start = pl.multiple_of((2 * z + side) * span, span)
        copies.append(
            (
                pltpu.make_async_copy(
                    hidden.at[:, pl.ds(start, span)], hidden_v.at[0, z], sems.at[0, z]
                ),
                pltpu.make_async_copy(
                    other.at[:, pl.ds(start, span)], hidden_v.at[1, z], sems.at[1, z]
                ),
                pltpu.make_async_copy(head.at[pl.ds(start, span), :], head_v.at[z], sems.at[2, z]),
            )
        )
        for copy in copies[-1]:
            copy.start()
    gain_f[...] = gain[...].astype(jnp.float32)
    owner = lax.broadcasted_iota(jnp.int32, (1, LANES), 1) // rows == place[1]
    moments[:rows, :] = first_w[...]
    moments[rows : 2 * rows, :] = second_w[...]
    for n, values in enumerate((first_g, second_g)):
        repeated = jnp.concatenate([values[...]] * (LANES // rows), axis=1)
        moments[2 * rows + n : 2 * rows + n + 1, :] = jnp.where(owner, repeated, 0.0)
    moments[2 * rows + 2 :, :] = jnp.zeros((6, LANES), jnp.float32)
    packs = (pack, other_pack)
    piece = 256
    errors, flipped, inv_rms = {}, {}, {}

    def prepare(g):
        values = packs[g][:tokens, :]
        flipped[g] = values.T.astype(jnp.bfloat16)
        errors[g] = values.astype(jnp.bfloat16)
        inv_rms[g] = jnp.concatenate(
            [packs[g][tokens : 2 * tokens, :]] * (piece // LANES), axis=1
        )

    prepare(1)
    blocks = width // LANES

    def spread(ref, first):
        return jnp.concatenate(
            [ref[pl.ds(first + m, 1), :] for m in range(piece // LANES)], axis=1
        )

    for z in range(size_z):
        for copy in copies[z]:
            copy.wait()
        for s in range(span // piece):
            lanes = slice(s * piece, (s + 1) * piece)
            first = (2 * z + side) * tiles + s * (piece // LANES)
            gain_row = spread(gain_f, first)
            weight = jnp.zeros((BINS, piece), jnp.float32)
            total = jnp.zeros((1, piece), jnp.float32)
            for g in (1, 0):
                if g not in errors:
                    own.wait()
                    prepare(g)
                back = lax.dot_general(
                    errors[g],
                    head_v[z, lanes, :],
                    (((1,), (1,)), ((), ())),
                    preferred_element_type=jnp.float32,
                )
                normed = hidden_v[g, z, :, lanes].astype(jnp.float32) * inv_rms[g]
                scaled = (normed * gain_row).astype(jnp.bfloat16)
                part = jnp.dot(flipped[g], scaled, preferred_element_type=jnp.float32)
                gain_part = jnp.sum(back * normed, axis=0, keepdims=True)
                limit = spread(packs[g], 2 * tokens + blocks + first)
                gain_q = jnp.clip(gain_part, -limit, limit).astype(jnp.bfloat16)
                total = total + gain_q.astype(jnp.float32)
                limit = spread(packs[g], 2 * tokens + first)
                weight_q = jnp.clip(part, -limit, limit).astype(jnp.bfloat16)
                weight = weight + weight_q.astype(jnp.float32)
            weight = weight.astype(jnp.bfloat16)
            for m in range(piece // LANES):
                turned = weight[:, m * LANES : (m + 1) * LANES].T
                tile = s * (piece // LANES) + m
                gain_sum[tile, z : z + 1, :] = total[:, m * LANES : (m + 1) * LANES]
                for n in range(LANES // rows):
                    out[tile * (LANES // rows) + n, z * rows : (z + 1) * rows, :] = turned[
                        n * rows : (n + 1) * rows, :
                    ]
    for m in range(tiles):
        high = gain_sum[m].astype(jnp.bfloat16)
        low = (gain_sum[m] - high.astype(jnp.float32)).astype(jnp.bfloat16)
        both = jnp.concatenate([high.astype(jnp.float32), low.astype(jnp.float32)], axis=0)
        for n in range(LANES // rows):
            out[m * (LANES // rows) + n, size_z * rows :, :] = both.astype(jnp.bfloat16)


def run_grads(place, hidden, other, head, gain, packs, moments, size_z, size_xy):
    tokens, width = hidden.shape
    span = width // (2 * size_z)
    rows = span // size_xy
    anywhere = pl.BlockSpec(memory_space=pl.ANY)
    vmem = pl.BlockSpec(memory_space=pltpu.VMEM)
    return pl.pallas_call(
        grads_kernel,
        out_shape=(
            jax.ShapeDtypeStruct((size_xy, size_z * rows + 2 * size_z, BINS), jnp.bfloat16),
            jax.ShapeDtypeStruct((2 * rows + 8, LANES), jnp.float32),
        ),
        in_specs=[pl.BlockSpec(memory_space=pltpu.SMEM)] + [anywhere] * 4 + [vmem] * 6,
        out_specs=(vmem, vmem),
        scratch_shapes=[
            pltpu.VMEM((2, size_z, tokens, span), jnp.bfloat16),
            pltpu.VMEM((size_z, span, BINS), jnp.bfloat16),
            pltpu.VMEM((width // LANES, LANES), jnp.float32),
            pltpu.VMEM((span // LANES, size_z, LANES), jnp.float32),
            pltpu.VMEM(packs[1].shape, jnp.float32),
            pltpu.SemaphoreType.DMA((3, size_z)),
            pltpu.SemaphoreType.DMA,
        ],
        cost_estimate=pl.CostEstimate(
            flops=4 * tokens * width * BINS, bytes_accessed=8 * width * tokens, transcendentals=0
        ),
        compiler_params=pltpu.CompilerParams(vmem_limit_bytes=53248 * 2**10),
        name="grads",
    )(place, hidden, other, head, packs[0], gain, packs[1], *moments)


def plane_kernel(parts, out):
    size_z = (parts.shape[1] - 2 * 8) // 32
    copies = out.shape[0] // size_z
    rows = 32
    total = parts[0].astype(jnp.float32)
    for n in range(1, parts.shape[0]):
        total = total + parts[n].astype(jnp.float32)
    for z in range(size_z):
        high_row = size_z * rows + z
        low_row = high_row + size_z
        gain = total[high_row : high_row + 1, :] + total[low_row : low_row + 1, :]
        high = gain.astype(jnp.bfloat16).astype(jnp.float32)
        block = jnp.concatenate(
            [
                total[z * rows : (z + 1) * rows, :],
                high,
                gain - high,
                jnp.zeros((6, LANES), jnp.float32),
            ],
            axis=0,
        ).astype(jnp.bfloat16)
        for n in range(copies):
            out[z * copies + n] = block


def run_plane(parts, size_z, size_pipe):
    vmem = pl.BlockSpec(memory_space=pltpu.VMEM)
    return pl.pallas_call(
        plane_kernel,
        out_shape=jax.ShapeDtypeStruct((size_z * size_pipe, 40, LANES), jnp.bfloat16),
        in_specs=[vmem],
        out_specs=vmem,
        compiler_params=pltpu.CompilerParams(vmem_limit_bytes=12 * 2**20),
        name="plane",
    )(parts)


def adam(param, grad, first, second):
    first_new = 0.9 * first + 0.1 * grad
    second_new = 0.95 * second + 0.05 * grad * grad
    update = first_new / FIRST_CORR / (jnp.sqrt(second_new / SECOND_CORR) + EPSILON)
    return param - LEARN_RATE * update, first_new, second_new


def update_kernel(
    place, parts, head, gain, own, next_1, next_2, next_3,
    new_weight, new_gain, first_w, second_w, first_g, second_g, weight_v, gain_f, sem,
):
    rows = first_w.shape[0]
    peers = LANES // rows
    size_z = parts.shape[0] // peers
    start = pl.multiple_of(place[2] * LANES, LANES)
    copy = pltpu.make_async_copy(head.at[pl.ds(start, LANES), :], weight_v, sem)
    copy.start()
    gain_f[...] = gain[...].astype(jnp.float32)
    moments = (own, next_1, next_2, next_3)
    grad = jnp.zeros((1, LANES), jnp.float32)
    for z in range(size_z):
        block = parts[z * peers].astype(jnp.float32)
        grad = grad + (block[rows : rows + 1, :] + block[rows + 1 : rows + 2, :])
    first, second = (
        sum(m[2 * rows + n : 2 * rows + n + 1, :] for m in moments[1:])
        + moments[0][2 * rows + n : 2 * rows + n + 1, :]
        for n in range(2)
    )
    updated, first, second = adam(gain_f[pl.ds(place[2], 1), :], grad, first, second)
    new_gain[...] = updated.astype(jnp.bfloat16)
    for ref, values in ((first_g, first), (second_g, second)):
        mine = jnp.zeros((1, rows), jnp.float32)
        for n in range(peers):
            mine = jnp.where(place[1] == n, values[:, n * rows : (n + 1) * rows], mine)
        ref[...] = mine
    copy.wait()
    for n in range(peers):
        peer = lax.rem(place[1] + n, peers)
        grad = jnp.zeros((rows, BINS), jnp.float32)
        for z in range(size_z):
            grad = grad + parts[z * peers + peer].astype(jnp.float32)[:rows, :]
        at = pl.multiple_of(peer * rows, rows)
        updated, first, second = adam(
            weight_v[pl.ds(at, rows), :].astype(jnp.float32),
            grad,
            moments[n][:rows, :],
            moments[n][rows : 2 * rows, :],
        )
        new_weight[pl.ds(at, rows), :] = updated.astype(jnp.bfloat16)
        if n == 0:
            first_w[...] = first
            second_w[...] = second


def run_update(place, parts, head, gain, moments):
    vmem = pl.BlockSpec(memory_space=pltpu.VMEM)
    rows = (moments[0].shape[0] - 8) // 2
    wide = jax.ShapeDtypeStruct((rows, BINS), jnp.float32)
    thin = jax.ShapeDtypeStruct((1, rows), jnp.float32)
    return pl.pallas_call(
        update_kernel,
        out_shape=(
            jax.ShapeDtypeStruct((LANES, BINS), jnp.bfloat16),
            jax.ShapeDtypeStruct((1, LANES), jnp.bfloat16),
            wide,
            wide,
            thin,
            thin,
        ),
        in_specs=[
            pl.BlockSpec(memory_space=pltpu.SMEM),
            vmem,
            pl.BlockSpec(memory_space=pl.ANY),
        ]
        + [vmem] * 5,
        out_specs=(vmem,) * 6,
        scratch_shapes=[
            pltpu.VMEM((LANES, BINS), jnp.bfloat16),
            pltpu.VMEM(gain.shape, jnp.float32),
            pltpu.SemaphoreType.DMA,
        ],
        compiler_params=pltpu.CompilerParams(vmem_limit_bytes=12 * 2**20),
        name="update",
    )(place, parts, head, gain, *moments)


def shards(
    final_hidden,
    value_head,
    norm_gain,
    rewards,
    old_values,
    loss_mask,
    row_exp,
    gain_exp,
    first_w,
    second_w,
    first_g,
    second_g,
):
    size_dp = lax.axis_size("dp")
    size_node = lax.axis_size("node")
    size_pipe = lax.axis_size("pipe")
    size_z = size_dp // 2
    size_xy = size_node * size_pipe
    rows = first_g.shape[0]
    tokens = final_hidden.shape[0]
    blocks = value_head.shape[0] // LANES
    dp, node, pipe = (lax.axis_index(name) for name in ("dp", "node", "pipe"))
    place = jnp.stack([lax.rem(dp, 2), pipe, dp * size_node + node]).astype(jnp.int32)
    swap = [(i, i ^ 1) for i in range(size_dp)]
    columns = [
        [((2 * z + c) * size_node + x) * size_pipe + y for z in range(size_z) for y in range(size_pipe)]
        for c in range(2)
        for x in range(size_node)
    ]

    other_hidden = lax.ppermute(final_hidden, "dp", swap)
    gain_blocks = norm_gain.reshape(blocks, LANES)
    pack, kept = run_forward(
        final_hidden,
        value_head,
        gain_blocks,
        rewards.reshape(1, tokens),
        old_values.reshape(1, tokens),
        loss_mask.reshape(1, tokens),
        row_exp,
        gain_exp,
    )
    other_pack = lax.ppermute(pack, "dp", swap)
    packed, moments = run_grads(
        place,
        final_hidden,
        other_hidden,
        value_head,
        gain_blocks,
        (kept, other_pack),
        (first_w, second_w, first_g.reshape(1, rows), second_g.reshape(1, rows)),
        size_z,
        size_xy,
    )
    packed = lax.all_to_all(packed, ("node", "pipe"), 0, 0, tiled=True)
    moments = [moments] + [
        lax.ppermute(moments, "pipe", [(i, (i - k) % size_pipe) for i in range(size_pipe)])
        for k in range(1, size_pipe)
    ]
    packed = run_plane(packed, size_z, size_pipe)
    packed = lax.all_to_all(
        packed, ("dp", "node", "pipe"), 0, 0, tiled=True, axis_index_groups=columns
    )
    new_weight, new_gain, first_w, second_w, first_g, second_g = run_update(
        place, packed, value_head, gain_blocks, moments
    )
    return (
        new_weight,
        new_gain.reshape(size_pipe * rows),
        first_w,
        second_w,
        first_g.reshape(rows),
        second_g.reshape(rows),
    )


def solution(mesh):
    return jax.shard_map(
        shards,
        mesh=mesh,
        in_specs=(
            P(("dp", "node", "pipe"), None),
            P(),
            P(),
            P(("dp", "node", "pipe")),
            P(("dp", "node", "pipe")),
            P(("dp", "node", "pipe")),
            P(("dp", "node", "pipe"), None),
            P(("dp", "node", "pipe"), None),
            P(("dp", "node", "pipe"), None),
            P(("dp", "node", "pipe"), None),
            P(("dp", "node", "pipe")),
            P(("dp", "node", "pipe")),
        ),
        out_specs=(
            P(("dp", "node"), None),
            P(("dp", "node")),
            P(("dp", "node", "pipe"), None),
            P(("dp", "node", "pipe"), None),
            P(("dp", "node", "pipe")),
            P(("dp", "node", "pipe")),
        ),
        check_vma=False,
    )
```
